512 devices in a mesh: wa: 64 (over y, x, z_hi), gz: 8 (over z_lo, core).
Axes of the slice: x: 4, y: 8, z: 8 (z_hi: 2, z_lo: 4; z = z_hi * 4 + z_lo), core: 2. Of those that a mesh axis runs over, the one named last changes fastest.
Arguments:
- wave: float32 [2, 8, 2048, 2048], P(None, 'gz', 'wa'), may hold values from -6 to 6
- potential: float32 [8, 2048, 2048], P('gz', 'wa'), may hold values from 0 to 800
Outputs:
- evolved: float32 [2, 8, 2048, 2048], P(None, 'gz', 'wa')
The draws below stay inside these ranges and needn't reach their ends.
All inputs are finite; a program needn't handle non-finite values.
Results may differ from the reference program's by a relative error of at most 0.0083.
Values may be sent and summed in bfloat16 or wider, within the bound.
No kernel may reach another device: no remote copies, remote signals or barrier semaphores. Data moves between devices by JAX's collectives and lax.ppermute only.
A program may use at most 64 MiB of HBM per device.

```python
import math
import jax
import jax.numpy as jnp
from jax import lax

GRID = 2048
NZ = 8


def levels(rng, shape, cuts, least, high):
    gain, own = 1.0, jax.random.fold_in(rng, 6)
    for position, parts in cuts:
        heights = jnp.exp(jax.random.uniform(jax.random.fold_in(own, position), (parts,), jnp.float32, least / len(cuts), high / len(cuts)))
        gain = gain * jnp.repeat(heights, shape[position] // parts).reshape([-1 if axis == position else 1 for axis in range(len(shape))])
    return gain


def gaussian(stream_key, shape, width, bound, shards=(), held_as=jnp.bfloat16):
    values = jax.random.normal(stream_key, shape, jnp.float32) * width
    if len(shards) > 0:
        values = levels(stream_key, shape, shards, -0.22, 0.18) * values
    return jnp.clip(values, min=-bound, max=bound).astype(held_as)


def setup_inputs(seed: int = 0) -> dict:
    key_list = jax.random.split(jax.random.key(seed), 3)
    wave = gaussian(key_list[0], (2, NZ, GRID, GRID), 1.0, 6.0, ((1, 8), (2, 64)), jnp.float32)
    potential = jnp.clip(800.0 * jax.random.uniform(key_list[1], (NZ, GRID, GRID), jnp.float32) ** levels(key_list[1], (NZ, GRID, GRID), ((0, 8), (1, 64)), -0.2, 0.2), 0.0, 800.0)
    return {"wave": wave, "potential": potential}


time_step = 0.001
spacing = 1.0 / 32.0
rotation = 0.9
coupling = 400.0
z_coupling = 0.25

def dft_tables(count):
    indices = jnp.arange(count, dtype=jnp.int32)
    residue = indices[:, None] * indices[None, :] % count
    angle = residue.astype(jnp.float32) * (2.0 * math.pi / count)
    weight = 1.0 / math.sqrt(count)
    cosine = (jnp.cos(angle) * weight).astype(jnp.bfloat16)
    sine = (jnp.sin(angle) * weight).astype(jnp.bfloat16)
    signed = jnp.where(indices < count // 2, indices, indices - count)
    wavenum = signed.astype(jnp.float32) * (2.0 * math.pi / (count * spacing))
    return (cosine, sine, wavenum)

def coordinates(first, count, total):
    steps_from = first + jnp.arange(count, dtype=jnp.int32) - total // 2
    return steps_from.astype(jnp.float32) * spacing

def spectral_phase(coords, wavenum, sign):
    return time_step * (0.5 * wavenum[None, :] * wavenum[None, :] + sign * rotation * coords[:, None] * wavenum[None, :])

def potential_step(wave, potential):
    real_part = wave[0]
    imag_part = wave[1]
    theta = time_step * (potential + coupling * (real_part * real_part + imag_part * imag_part))
    cos_theta = jnp.cos(theta)
    sin_theta = jnp.sin(theta)
    return jnp.stack([real_part * cos_theta + imag_part * sin_theta, imag_part * cos_theta - real_part * sin_theta])

def apply_table(values, table):
    return jnp.dot(values, table, preferred_element_type=jnp.float32)

def sweep_plane(field, phase, cosine, sine):
    lowered = field.astype(jnp.bfloat16)
    spec_real = apply_table(lowered[0], cosine) + apply_table(lowered[1], sine)
    spec_imag = apply_table(lowered[1], cosine) - apply_table(lowered[0], sine)
    turn_cos = jnp.cos(phase)
    turn_sin = jnp.sin(phase)
    rot_real = (spec_real * turn_cos + spec_imag * turn_sin).astype(jnp.bfloat16)
    rot_imag = (spec_imag * turn_cos - spec_real * turn_sin).astype(jnp.bfloat16)
    out_real = apply_table(rot_real, cosine) - apply_table(rot_imag, sine)
    out_imag = apply_table(rot_imag, cosine) + apply_table(rot_real, sine)
    return jnp.stack([out_real, out_imag])

def sweep_all(field, phase, cosine, sine):
    planes = jnp.moveaxis(field, 1, 0)
    swept = lax.map(lambda single_plane: sweep_plane(single_plane, phase, cosine, sine), planes)
    return jnp.moveaxis(swept, 0, 1)

def zero_extend(values):
    return jnp.pad(values, ((0, 0), (1, 1), (0, 0), (0, 0)))

def second_difference(values, padded):
    return padded[:, 2:] + padded[:, :-2] - 2.0 * values

def z_step(field, extend):
    first_term = -z_coupling * second_difference(field, extend(field))
    second_term = -z_coupling * second_difference(first_term, extend(first_term))
    new_real = field[0] + first_term[1] - 0.5 * second_term[0]
    new_imag = field[1] - first_term[0] - 0.5 * second_term[1]
    return jnp.stack([new_real, new_imag])

def reference(wave, potential):
    cosine, sine, wavenum = dft_tables(GRID)
    field = potential_step(wave, potential)
    coords = coordinates(0, GRID, GRID)
    field = sweep_all(field, spectral_phase(coords, wavenum, 1.0), cosine, sine)
    field = jnp.swapaxes(field.astype(jnp.bfloat16), 2, 3)
    field = sweep_all(field, spectral_phase(coords, wavenum, -1.0), cosine, sine)
    return z_step(field, zero_extend)
```

```python
import math

import jax
import jax.numpy as jnp
import numpy as np
from jax import lax
from jax.experimental import pallas as pl
from jax.experimental.pallas import tpu as pltpu
from jax.sharding import PartitionSpec as P

time_step = 0.001
spacing = 1.0 / 32.0
rotation = 0.9
coupling = 400.0
z_coupling = 0.25

GRID = 2048
LANES = 128
COLS = 16
ROWS = 32
GROUPS = 4
PARTS_WA = 64

NEAR = (2.0 * z_coupling * z_coupling, z_coupling)
FAR = -0.5 * z_coupling * z_coupling
CENTRE = (1.0 - 3.0 * z_coupling * z_coupling, -2.0 * z_coupling)
CENTRE_EDGE = 1.0 - 2.5 * z_coupling * z_coupling


def tables():
    lane = np.arange(LANES)
    turned_lane = 32 * ((lane // 8) % 4) + 8 * (lane // 32) + lane % 8
    scale = 1.0 / math.sqrt(GRID)

    def matrices(order):
        angle = 2.0 * np.pi * ((order[:, None] * lane[None, :]) % LANES) / LANES
        cos, sin = np.cos(angle) * scale, np.sin(angle) * scale
        forward = np.block([[cos, -sin], [sin, cos]])
        return forward

    def split(matrix):
        high = matrix.astype(jnp.bfloat16)
        low = (matrix - high.astype(np.float64)).astype(jnp.bfloat16)
        return np.stack([np.asarray(high), np.asarray(low)])

    def twiddle(order):
        angle = 2.0 * np.pi * np.arange(COLS)[:, None] * order[None, :] / GRID
        return np.stack([np.cos(angle), np.sin(angle)]).astype(np.float32)

    angle = 2.0 * np.pi * ((lane[:, None] * lane[None, :]) % LANES) / LANES
    cos, sin = np.cos(angle) * scale, np.sin(angle) * scale
    backward = split(np.block([[cos, sin], [-sin, cos]]))
    mode = np.arange(COLS)[:, None] + COLS * lane[None, :]
    signed = np.where(mode < GRID // 2, mode, mode - GRID).astype(np.float64)
    wavenum = signed * (2.0 * np.pi / (GRID * spacing))
    slope = time_step * rotation * spacing * wavenum
    rows8 = slope[:, None, :] * np.arange(8)[None, :, None]
    own = np.stack([np.cos(rows8), np.sin(rows8)]).astype(np.float32)
    step8 = np.stack([np.cos(8.0 * slope), np.sin(8.0 * slope)]).astype(np.float32)
    return {
        "fwd_x": split(matrices(lane)),
        "fwd_y": split(matrices(turned_lane)),
        "inv": backward,
        "tw_x": twiddle(lane),
        "tw_y": twiddle(turned_lane),
        "wavenum": wavenum.astype(np.float32),
        "own": own,
        "step8": step8,
    }


def sincos(angle):
    turns = jnp.floor(angle * (2.0 / math.pi) + 0.5)
    rest = angle - turns * 1.5703125
    rest = rest - turns * 4.837512969970703e-4
    rest = rest - turns * 7.54978995489188e-8
    square = rest * rest
    sine = rest + rest * square * (
        -1.6666654611e-1 + square * (8.3321608736e-3 - square * 1.9515295891e-4)
    )
    cosine = 1.0 - 0.5 * square + square * square * (
        4.166664568298827e-2 + square * (-1.388731625493765e-3 + square * 2.443315711809948e-5)
    )
    quadrant = turns.astype(jnp.int32)
    swapped = (quadrant & 1) == 1
    sin_out = jnp.where(swapped, cosine, sine)
    cos_out = jnp.where(swapped, sine, cosine)
    sin_out = jnp.where((quadrant & 2) == 2, -sin_out, sin_out)
    cos_out = jnp.where(((quadrant + 1) & 2) == 2, -cos_out, cos_out)
    return sin_out, cos_out


def dft4(v, sign):
    (ar, ai), (br, bi), (cr, ci), (dr, di) = v
    sr, si, tr, ti = ar + cr, ai + ci, ar - cr, ai - ci
    ur, ui, wr, wi = br + dr, bi + di, br - dr, bi - di
    if sign > 0:
        p, q = (tr + wi, ti - wr), (tr - wi, ti + wr)
    else:
        p, q = (tr - wi, ti + wr), (tr + wi, ti - wr)
    return [(sr + ur, si + ui), p, (sr - ur, si - ui), q]


def turn16(v, power, sign):
    power %= 16
    re, im = v
    if power == 0:
        return v
    c, s = math.cos(2.0 * math.pi * power / 16), -sign * math.sin(2.0 * math.pi * power / 16)
    if power == 4:
        return (im, -re) if sign > 0 else (-im, re)
    if power % 2 == 0:
        h = math.sqrt(0.5)
        return (h * (_pm(re, c) + _pm(im, -s)), h * (_pm(re, s) + _pm(im, c)))
    return (re * c - im * s, re * s + im * c)


def _pm(x, sign):
    return x if sign > 0 else -x


def dft16(v, sign):
    low = [dft4([v[4 * a + b] for a in range(4)], sign) for b in range(4)]
    out = [None] * 16
    for k in range(4):
        high = dft4([turn16(low[b][k], b * k, sign) for b in range(4)], sign)
        for k2 in range(4):
            out[k + 4 * k2] = high[k2]
    return out


def swap_blocks(v):
    lane = lax.broadcasted_iota(jnp.int32, (8, LANES), 1)

    def stage(first, second, width):
        upper = (lane // width) % 2 == 1
        a = jnp.where(upper, pltpu.roll(second, width, 1), first)
        b = jnp.where(upper, second, pltpu.roll(first, LANES - width, 1))
        return a, b

    v0, v2 = stage(v[0], v[2], 64)
    v1, v3 = stage(v[1], v[3], 64)
    v0, v1 = stage(v0, v1, 32)
    v2, v3 = stage(v2, v3, 32)
    return [v0, v1, v2, v3]


def row_phases(first_row, wavenum, step8, sign):
    angle = time_step * (0.5 * wavenum * wavenum + (sign * rotation * first_row) * wavenum)
    sine, cosine = sincos(angle)
    re, im = cosine, -sine
    sr, si = step8[0], -sign * step8[1]
    out = [(re, im)]
    for _ in range(GROUPS - 1):
        re, im = re * sr - im * si, re * si + im * sr
        out.append((re, im))
    return out


def double_dot(left, table_ref):
    return jnp.dot(left, table_ref[0], preferred_element_type=jnp.float32) + jnp.dot(
        left, table_ref[1], preferred_element_type=jnp.float32
    )


def sweep(load, store, first_row, fwd_ref, inv_ref, tw_f_ref, tw_i_ref, wave_ref, own_ref, step_ref, buf, sign):
    for g in range(GROUPS):
        rows = slice(8 * g, 8 * g + 8)
        out = dft16([load(g, c) for c in range(COLS)], 1)
        for m in range(COLS):
            re, im = out[m]
            if m > 0:
                c, s = tw_f_ref[0, m : m + 1, :], tw_f_ref[1, m : m + 1, :]
                re, im = re * c + im * s, im * c - re * s
            buf[m, rows, :LANES] = re
            buf[m, rows, LANES:] = im
    spectrum = double_dot(buf[...].reshape(COLS * ROWS, 2 * LANES).astype(jnp.bfloat16), fwd_ref)
    buf[...] = spectrum.reshape(COLS, ROWS, 2 * LANES)
    phases = row_phases(first_row, wave_ref[...], step_ref[...], sign)
    for m in range(COLS):
        own_re, own_im = own_ref[0, m], -sign * own_ref[1, m]
        for g in range(GROUPS):
            rows = slice(8 * g, 8 * g + 8)
            row_re, row_im = phases[g][0][m : m + 1, :], phases[g][1][m : m + 1, :]
            f_re, f_im = own_re * row_re - own_im * row_im, own_re * row_im + own_im * row_re
            re, im = buf[m, rows, :LANES], buf[m, rows, LANES:]
            buf[m, rows, :LANES] = re * f_re - im * f_im
            buf[m, rows, LANES:] = re * f_im + im * f_re
    turned = double_dot(buf[...].reshape(COLS * ROWS, 2 * LANES).astype(jnp.bfloat16), inv_ref)
    buf[...] = turned.reshape(COLS, ROWS, 2 * LANES)
    for g in range(GROUPS):
        rows = slice(8 * g, 8 * g + 8)
        terms = []
        for m in range(COLS):
            re, im = buf[m, rows, :LANES], buf[m, rows, LANES:]
            if m > 0:
                c, s = tw_i_ref[0, m : m + 1, :], tw_i_ref[1, m : m + 1, :]
                re, im = re * c - im * s, im * c + re * s
            terms.append((re, im))
        for c, (re, im) in enumerate(dft16(terms, -1)):
            store(g, c, re, im)


def potential_kernel(wave_ref, potential_ref, out_ref):
    for g in range(2):
        rows = slice(16 * g, 16 * g + 16)
        for c in range(COLS):
            at = slice(LANES * c, LANES * c + LANES)
            re, im, pot = wave_ref[0, 0, rows, at], wave_ref[1, 0, rows, at], potential_ref[0, rows, at]
            sine, cosine = sincos(time_step * (pot + coupling * (re * re + im * im)))
            out_ref[0, rows, at] = (re * cosine + im * sine).astype(jnp.bfloat16)
            out_ref[1, rows, at] = (im * cosine - re * sine).astype(jnp.bfloat16)


def x_kernel(scalar_ref, own_ref, pair_ref, left_ref, right_ref, fwd_ref, inv_ref, tw_ref, wave_ref, rows_ref, step_ref, out_ref, mixed, buf, swept):
    centre = scalar_ref[1]
    for g in range(2):
        rows = slice(16 * g, 16 * g + 16)
        for c in range(COLS):
            at = slice(LANES * c, LANES * c + LANES)
            re, im, pre, pim, lre, lim, rre, rim = (
                ref[p, rows, at].astype(jnp.float32)
                for ref in (own_ref, pair_ref, left_ref, right_ref)
                for p in range(2)
            )
            mixed[0, rows, at] = centre * re - CENTRE[1] * im + (NEAR[0] * pre - NEAR[1] * pim) + (lre + rre)
            mixed[1, rows, at] = centre * im + CENTRE[1] * re + (NEAR[0] * pim + NEAR[1] * pre) + (lim + rim)

    def load(g, c):
        at = slice(LANES * c, LANES * c + LANES)
        return mixed[0, 8 * g : 8 * g + 8, at], mixed[1, 8 * g : 8 * g + 8, at]

    def store(g, c, re, im):
        swept[c, 0, g] = re
        swept[c, 1, g] = im

    sweep(load, store, scalar_ref[0], fwd_ref, inv_ref, tw_ref, tw_ref, wave_ref, rows_ref, step_ref, buf, 1.0)
    for c in range(COLS):
        re = swap_blocks([swept[c, 0, g] for g in range(GROUPS)])
        im = swap_blocks([swept[c, 1, g] for g in range(GROUPS)])
        for q in range(4):
            out_ref[4 * c + q] = jnp.concatenate([re[q], im[q]], axis=0).astype(jnp.bfloat16)


def y_kernel(scalar_ref, in_ref, fwd_ref, inv_ref, tw_f_ref, tw_i_ref, wave_ref, rows_ref, step_ref, out_ref, field, buf):
    for s in range(4):
        block = in_ref[16 * s : 16 * s + 16].astype(jnp.float32)
        for p in range(2):
            flipped = jnp.transpose(block[:, 8 * p : 8 * p + 8, :].reshape(LANES, LANES))
            for x in range(4):
                parts = swap_blocks([flipped[32 * g + 8 * x : 32 * g + 8 * x + 8] for g in range(4)])
                for a in range(4):
                    field[p, 8 * x : 8 * x + 8, LANES * (4 * s + a) : LANES * (4 * s + a + 1)] = parts[a]

    def load(g, c):
        at = slice(LANES * c, LANES * c + LANES)
        return field[0, 8 * g : 8 * g + 8, at], field[1, 8 * g : 8 * g + 8, at]

    def store(g, c, re, im):
        at = slice(LANES * c, LANES * c + LANES)
        out_ref[0, 0, 8 * g : 8 * g + 8, at] = re
        out_ref[1, 0, 8 * g : 8 * g + 8, at] = im

    sweep(load, store, scalar_ref[0], fwd_ref, inv_ref, tw_f_ref, tw_i_ref, wave_ref, rows_ref, step_ref, buf, -1.0)


SMEM = pl.BlockSpec(memory_space=pltpu.SMEM)
VMEM = pl.BlockSpec(memory_space=pltpu.VMEM)
PARAMS = pltpu.CompilerParams(vmem_limit_bytes=48 * 1024 * 1024)


def on_device(wave, potential):
    t = tables()
    f32, bf16 = jnp.float32, jnp.bfloat16
    row_base = lax.axis_index("wa") * ROWS - GRID // 2
    plane = lax.axis_index("gz")
    edge = (plane == 0) | (plane == 7)
    odd = (plane % 2).astype(f32)
    scalars = jnp.stack([row_base.astype(f32) * spacing, jnp.where(edge, CENTRE_EDGE, CENTRE[0])])
    own = pl.pallas_call(
        potential_kernel,
        out_shape=jax.ShapeDtypeStruct((2, ROWS, GRID), bf16),
        in_specs=[VMEM, VMEM],
        out_specs=VMEM,
        compiler_params=PARAMS,
    )(wave, potential)
    pair = lax.ppermute(own, "gz", [(i, i ^ 1) for i in range(8)])
    far = FAR * own.astype(f32)
    pr, pi = pair[0].astype(f32), pair[1].astype(f32)
    near = jnp.stack([NEAR[0] * pr - NEAR[1] * pi, NEAR[0] * pi + NEAR[1] * pr])
    to_right = (far + (1.0 - odd) * near).astype(bf16)
    to_left = (far + odd * near).astype(bf16)
    left = lax.ppermute(to_right, "gz", [(i, i + 2) for i in range(6)])
    right = lax.ppermute(to_left, "gz", [(i + 2, i) for i in range(6)])
    chunks = pl.pallas_call(
        x_kernel,
        out_shape=jax.ShapeDtypeStruct((PARTS_WA, 16, LANES), bf16),
        in_specs=[SMEM] + [VMEM] * 10,
        out_specs=VMEM,
        scratch_shapes=[
            pltpu.VMEM((2, ROWS, GRID), f32),
            pltpu.VMEM((COLS, ROWS, 2 * LANES), f32),
            pltpu.VMEM((COLS, 2, GROUPS, 8, LANES), f32),
        ],
        compiler_params=PARAMS,
    )(scalars, own, pair, left, right, t["fwd_x"], t["inv"], t["tw_x"], t["wavenum"], t["own"], t["step8"])
    chunks = lax.all_to_all(chunks, "wa", 0, 0, tiled=True)
    return pl.pallas_call(
        y_kernel,
        out_shape=jax.ShapeDtypeStruct((2, 1, ROWS, GRID), f32),
        in_specs=[SMEM] + [VMEM] * 8,
        out_specs=VMEM,
        scratch_shapes=[
            pltpu.VMEM((2, ROWS, GRID), f32),
            pltpu.VMEM((COLS, ROWS, 2 * LANES), f32),
        ],
        compiler_params=PARAMS,
    )(scalars, chunks, t["fwd_y"], t["inv"], t["tw_y"], t["tw_x"], t["wavenum"], t["own"], t["step8"])


def solution(mesh):
    in_specs = (P(None, "gz", "wa", None), P("gz", "wa", None))
    out_specs = P(None, "gz", "wa", None)
    return jax.shard_map(
        on_device, mesh=mesh, in_specs=in_specs, out_specs=out_specs, check_vma=False
    )
```

```python
import math

import jax
import jax.numpy as jnp
import numpy as np
from jax import lax
from jax.experimental import pallas as pl
from jax.experimental.pallas import tpu as pltpu
from jax.sharding import PartitionSpec as P

time_step = 0.001
spacing = 1.0 / 32.0
rotation = 0.9
coupling = 400.0
z_coupling = 0.25

GRID = 2048
LANES = 128
COLS = 16
ROWS = 32
GROUPS = 4
PARTS_WA = 64

NEAR = (2.0 * z_coupling * z_coupling, z_coupling)
FAR = -0.5 * z_coupling * z_coupling
CENTRE = (1.0 - 3.0 * z_coupling * z_coupling, -2.0 * z_coupling)
CENTRE_EDGE = 1.0 - 2.5 * z_coupling * z_coupling


def tables():
    lane = np.arange(LANES)
    turned_lane = 32 * ((lane // 8) % 4) + 8 * (lane // 32) + lane % 8
    scale = 1.0 / math.sqrt(GRID)

    def matrices(order):
        angle = 2.0 * np.pi * ((order[:, None] * lane[None, :]) % LANES) / LANES
        cos, sin = np.cos(angle) * scale, np.sin(angle) * scale
        forward = np.block([[cos, -sin], [sin, cos]])
        return forward

    def split(matrix):
        high = matrix.astype(jnp.bfloat16)
        low = (matrix - high.astype(np.float64)).astype(jnp.bfloat16)
        return np.stack([np.asarray(high), np.asarray(low)])

    def twiddle(order):
        angle = 2.0 * np.pi * np.arange(COLS)[:, None] * order[None, :] / GRID
        return np.stack([np.cos(angle), np.sin(angle)]).astype(np.float32)

    angle = 2.0 * np.pi * ((lane[:, None] * lane[None, :]) % LANES) / LANES
    cos, sin = np.cos(angle) * scale, np.sin(angle) * scale
    backward = split(np.block([[cos, sin], [-sin, cos]]))
    mode = np.arange(COLS)[:, None] + COLS * lane[None, :]
    signed = np.where(mode < GRID // 2, mode, mode - GRID).astype(np.float64)
    wavenum = signed * (2.0 * np.pi / (GRID * spacing))
    slope = time_step * rotation * spacing * wavenum
    rows8 = slope[:, None, :] * np.arange(8)[None, :, None]
    own = np.stack([np.cos(rows8), np.sin(rows8)]).astype(np.float32)
    step8 = np.stack([np.cos(8.0 * slope), np.sin(8.0 * slope)]).astype(np.float32)
    return {
        "fwd_x": split(matrices(lane)),
        "fwd_y": split(matrices(turned_lane)),
        "inv": backward,
        "tw_x": twiddle(lane),
        "tw_y": twiddle(turned_lane),
        "wavenum": wavenum.astype(np.float32),
        "own": own,
        "step8": step8,
    }


def sincos(angle):
    turns = jnp.floor(angle * (2.0 / math.pi) + 0.5)
    rest = angle - turns * 1.5703125
    rest = rest - turns * 4.837512969970703e-4
    rest = rest - turns * 7.54978995489188e-8
    square = rest * rest
    sine = rest + rest * square * (
        -1.6666654611e-1 + square * (8.3321608736e-3 - square * 1.9515295891e-4)
    )
    cosine = 1.0 - 0.5 * square + square * square * (
        4.166664568298827e-2 + square * (-1.388731625493765e-3 + square * 2.443315711809948e-5)
    )
    quadrant = turns.astype(jnp.int32)
    swapped = (quadrant & 1) == 1
    sin_out = jnp.where(swapped, cosine, sine)
    cos_out = jnp.where(swapped, sine, cosine)
    sin_out = jnp.where((quadrant & 2) == 2, -sin_out, sin_out)
    cos_out = jnp.where(((quadrant + 1) & 2) == 2, -cos_out, cos_out)
    return sin_out, cos_out


def dft4(v, sign):
    (ar, ai), (br, bi), (cr, ci), (dr, di) = v
    sr, si, tr, ti = ar + cr, ai + ci, ar - cr, ai - ci
    ur, ui, wr, wi = br + dr, bi + di, br - dr, bi - di
    if sign > 0:
        p, q = (tr + wi, ti - wr), (tr - wi, ti + wr)
    else:
        p, q = (tr - wi, ti + wr), (tr + wi, ti - wr)
    return [(sr + ur, si + ui), p, (sr - ur, si - ui), q]


def turn16(v, power, sign):
    power %= 16
    re, im = v
    if power == 0:
        return v
    c, s = math.cos(2.0 * math.pi * power / 16), -sign * math.sin(2.0 * math.pi * power / 16)
    if power == 4:
        return (im, -re) if sign > 0 else (-im, re)
    if power % 2 == 0:
        h = math.sqrt(0.5)
        return (h * (_pm(re, c) + _pm(im, -s)), h * (_pm(re, s) + _pm(im, c)))
    return (re * c - im * s, re * s + im * c)


def _pm(x, sign):
    return x if sign > 0 else -x


def dft16(v, sign):
    low = [dft4([v[4 * a + b] for a in range(4)], sign) for b in range(4)]
    out = [None] * 16
    for k in range(4):
        high = dft4([turn16(low[b][k], b * k, sign) for b in range(4)], sign)
        for k2 in range(4):
            out[k + 4 * k2] = high[k2]
    return out


def swap_blocks(v):
    lane = lax.broadcasted_iota(jnp.int32, (8, LANES), 1)

    def stage(first, second, width):
        upper = (lane // width) % 2 == 1
        a = jnp.where(upper, pltpu.roll(second, width, 1), first)
        b = jnp.where(upper, second, pltpu.roll(first, LANES - width, 1))
        return a, b

    v0, v2 = stage(v[0], v[2], 64)
    v1, v3 = stage(v[1], v[3], 64)
    v0, v1 = stage(v0, v1, 32)
    v2, v3 = stage(v2, v3, 32)
    return [v0, v1, v2, v3]


def row_phases(first_row, wavenum, step8, sign):
    angle = time_step * (0.5 * wavenum * wavenum + (sign * rotation * first_row) * wavenum)
    sine, cosine = sincos(angle)
    re, im = cosine, -sine
    sr, si = step8[0], -sign * step8[1]
    out = [(re, im)]
    for _ in range(GROUPS - 1):
        re, im = re * sr - im * si, re * si + im * sr
        out.append((re, im))
    return out


def double_dot(left, table_ref):
    return jnp.dot(left, table_ref[0], preferred_element_type=jnp.float32) + jnp.dot(
        left, table_ref[1], preferred_element_type=jnp.float32
    )


def sweep(load, store, first_row, fwd_ref, inv_ref, tw_f_ref, tw_i_ref, wave_ref, own_ref, step_ref, buf, sign, finish=None):
    for g in range(GROUPS):
        rows = slice(8 * g, 8 * g + 8)
        out = dft16([load(g, c) for c in range(COLS)], 1)
        for m in range(COLS):
            re, im = out[m]
            if m > 0:
                c, s = tw_f_ref[0, m : m + 1, :], tw_f_ref[1, m : m + 1, :]
                re, im = re * c + im * s, im * c - re * s
            buf[m, rows, :LANES] = re
            buf[m, rows, LANES:] = im
    spectrum = double_dot(buf[...].reshape(COLS * ROWS, 2 * LANES).astype(jnp.bfloat16), fwd_ref)
    buf[...] = spectrum.reshape(COLS, ROWS, 2 * LANES)
    phases = row_phases(first_row, wave_ref[...], step_ref[...], sign)
    for m in range(COLS):
        own_re, own_im = own_ref[0, m], -sign * own_ref[1, m]
        for g in range(GROUPS):
            rows = slice(8 * g, 8 * g + 8)
            row_re, row_im = phases[g][0][m : m + 1, :], phases[g][1][m : m + 1, :]
            f_re, f_im = own_re * row_re - own_im * row_im, own_re * row_im + own_im * row_re
            re, im = buf[m, rows, :LANES], buf[m, rows, LANES:]
            buf[m, rows, :LANES] = re * f_re - im * f_im
            buf[m, rows, LANES:] = re * f_im + im * f_re
    turned = double_dot(buf[...].reshape(COLS * ROWS, 2 * LANES).astype(jnp.bfloat16), inv_ref)
    buf[...] = turned.reshape(COLS, ROWS, 2 * LANES)
    for g in range(GROUPS):
        rows = slice(8 * g, 8 * g + 8)
        terms = []
        for m in range(COLS):
            re, im = buf[m, rows, :LANES], buf[m, rows, LANES:]
            if m > 0:
                c, s = tw_i_ref[0, m : m + 1, :], tw_i_ref[1, m : m + 1, :]
                re, im = re * c - im * s, im * c + re * s
            terms.append((re, im))
        for c, (re, im) in enumerate(dft16(terms, -1)):
            store(g, c, re, im)
        if finish is not None:
            finish(g)


def potential_kernel(wave_hbm, potential_hbm, out_ref, wave_ref, potential_ref, sems):
    half = GRID // 2
    blocks = [(slice(16 * g, 16 * g + 16), slice(half * h, half * h + half)) for g in range(2) for h in range(2)]
    copies = []
    for b, (rows, at) in enumerate(blocks):
        copies.append([
            pltpu.make_async_copy(wave_hbm.at[0, 0, rows, at], wave_ref.at[0, rows, at], sems.at[b, 0]),
            pltpu.make_async_copy(wave_hbm.at[1, 0, rows, at], wave_ref.at[1, rows, at], sems.at[b, 1]),
            pltpu.make_async_copy(potential_hbm.at[0, rows, at], potential_ref.at[rows, at], sems.at[b, 2]),
        ])
        for copy in copies[-1]:
            copy.start()
    for (rows, at), waits in zip(blocks, copies):
        for copy in waits:
            copy.wait()
        for first in range(at.start, at.stop, LANES):
            cols = slice(first, first + LANES)
            re, im, pot = wave_ref[0, rows, cols], wave_ref[1, rows, cols], potential_ref[rows, cols]
            sine, cosine = sincos(time_step * (pot + coupling * (re * re + im * im)))
            out_ref[0, rows, cols] = (re * cosine + im * sine).astype(jnp.bfloat16)
            out_ref[1, rows, cols] = (im * cosine - re * sine).astype(jnp.bfloat16)


def message_kernel(own_ref, pair_ref, out_ref):
    for g in range(2):
        rows = slice(16 * g, 16 * g + 16)
        for c in range(COLS):
            at = slice(LANES * c, LANES * c + LANES)
            re, im, pre, pim = (ref[p, rows, at].astype(jnp.float32) for ref in (own_ref, pair_ref) for p in range(2))
            out_ref[0, rows, at] = (FAR * re + NEAR[0] * pre - NEAR[1] * pim).astype(jnp.bfloat16)
            out_ref[1, rows, at] = (FAR * im + NEAR[0] * pim + NEAR[1] * pre).astype(jnp.bfloat16)


def x_kernel(scalar_ref, own_ref, pair_ref, far_ref, sum_ref, fwd_ref, inv_ref, tw_ref, wave_ref, rows_ref, step_ref, out_ref, mixed, buf, swept):
    centre = scalar_ref[1]
    for g in range(2):
        rows = slice(16 * g, 16 * g + 16)
        for c in range(COLS):
            at = slice(LANES * c, LANES * c + LANES)
            re, im, pre, pim, fre, fim, sre, sim = (
                ref[p, rows, at].astype(jnp.float32)
                for ref in (own_ref, pair_ref, far_ref, sum_ref)
                for p in range(2)
            )
            mixed[0, rows, at] = centre * re - CENTRE[1] * im + (NEAR[0] * pre - NEAR[1] * pim) + (FAR * fre + sre)
            mixed[1, rows, at] = centre * im + CENTRE[1] * re + (NEAR[0] * pim + NEAR[1] * pre) + (FAR * fim + sim)

    def load(g, c):
        at = slice(LANES * c, LANES * c + LANES)
        return mixed[0, 8 * g : 8 * g + 8, at], mixed[1, 8 * g : 8 * g + 8, at]

    def store(g, c, re, im):
        swept[c, 0, g] = re
        swept[c, 1, g] = im

    sweep(load, store, scalar_ref[0], fwd_ref, inv_ref, tw_ref, tw_ref, wave_ref, rows_ref, step_ref, buf, 1.0)
    for c in range(COLS):
        re = swap_blocks([swept[c, 0, g] for g in range(GROUPS)])
        im = swap_blocks([swept[c, 1, g] for g in range(GROUPS)])
        for q in range(4):
            out_ref[4 * c + q] = jnp.concatenate([re[q], im[q]], axis=0).astype(jnp.bfloat16)


def y_kernel(scalar_ref, in_ref, fwd_ref, inv_ref, tw_f_ref, tw_i_ref, wave_ref, rows_ref, step_ref, out_hbm, field, buf, out_ref, sems):
    for s in range(4):
        block = in_ref[16 * s : 16 * s + 16].astype(jnp.float32)
        for p in range(2):
            flipped = jnp.transpose(block[:, 8 * p : 8 * p + 8, :].reshape(LANES, LANES))
            for x in range(4):
                parts = swap_blocks([flipped[32 * g + 8 * x : 32 * g + 8 * x + 8] for g in range(4)])
                for a in range(4):
                    field[p, 8 * x : 8 * x + 8, LANES * (4 * s + a) : LANES * (4 * s + a + 1)] = parts[a]

    def load(g, c):
        at = slice(LANES * c, LANES * c + LANES)
        return field[0, 8 * g : 8 * g + 8, at], field[1, 8 * g : 8 * g + 8, at]

    def store(g, c, re, im):
        at = slice(LANES * c, LANES * c + LANES)
        out_ref[0, 8 * g : 8 * g + 8, at] = re
        out_ref[1, 8 * g : 8 * g + 8, at] = im

    copies = []

    def send(g):
        rows = slice(8 * g, 8 * g + 8)
        for p in range(2):
            copies.append(pltpu.make_async_copy(out_ref.at[p, rows], out_hbm.at[p, 0, rows], sems.at[g, p]))
            copies[-1].start()

    sweep(load, store, scalar_ref[0], fwd_ref, inv_ref, tw_f_ref, tw_i_ref, wave_ref, rows_ref, step_ref, buf, -1.0, send)
    for copy in copies:
        copy.wait()


SMEM = pl.BlockSpec(memory_space=pltpu.SMEM)
HBM = pl.BlockSpec(memory_space=pltpu.HBM)
VMEM = pl.BlockSpec(memory_space=pltpu.VMEM)
PARAMS = pltpu.CompilerParams(vmem_limit_bytes=48 * 1024 * 1024)


def on_device(wave, potential):
    t = tables()
    f32, bf16 = jnp.float32, jnp.bfloat16
    row_base = lax.axis_index("wa") * ROWS - GRID // 2
    plane = lax.axis_index("gz")
    edge = (plane == 0) | (plane == 7)
    scalars = jnp.stack([row_base.astype(f32) * spacing, jnp.where(edge, CENTRE_EDGE, CENTRE[0])])
    own = pl.pallas_call(
        potential_kernel,
        out_shape=jax.ShapeDtypeStruct((2, ROWS, GRID), bf16),
        in_specs=[HBM, HBM],
        out_specs=VMEM,
        scratch_shapes=[
            pltpu.VMEM((2, ROWS, GRID), f32),
            pltpu.VMEM((ROWS, GRID), f32),
            pltpu.SemaphoreType.DMA((4, 3)),
        ],
        compiler_params=PARAMS,
    )(pltpu.with_memory_space_constraint(wave, pltpu.HBM), pltpu.with_memory_space_constraint(potential, pltpu.HBM))
    far = lax.ppermute(own, "gz", [(i, i - 2) for i in (2, 4, 6)] + [(i, i + 2) for i in (1, 3, 5)])
    pair = lax.ppermute(own, "gz", [(i, i ^ 1) for i in range(8)])
    message = pl.pallas_call(
        message_kernel,
        out_shape=jax.ShapeDtypeStruct((2, ROWS, GRID), bf16),
        in_specs=[VMEM, VMEM],
        out_specs=VMEM,
        compiler_params=PARAMS,
    )(own, pair)
    summed = lax.ppermute(message, "gz", [(i, i + 2) for i in (0, 2, 4)] + [(i, i - 2) for i in (3, 5, 7)])
    chunks = pl.pallas_call(
        x_kernel,
        out_shape=jax.ShapeDtypeStruct((PARTS_WA, 16, LANES), bf16),
        in_specs=[SMEM] + [VMEM] * 10,
        out_specs=VMEM,
        scratch_shapes=[
            pltpu.VMEM((2, ROWS, GRID), f32),
            pltpu.VMEM((COLS, ROWS, 2 * LANES), f32),
            pltpu.VMEM((COLS, 2, GROUPS, 8, LANES), f32),
        ],
        compiler_params=PARAMS,
    )(scalars, own, pair, far, summed, t["fwd_x"], t["inv"], t["tw_x"], t["wavenum"], t["own"], t["step8"])
    chunks = lax.all_to_all(chunks, "wa", 0, 0, tiled=True)
    return pl.pallas_call(
        y_kernel,
        out_shape=jax.ShapeDtypeStruct((2, 1, ROWS, GRID), f32),
        in_specs=[SMEM] + [VMEM] * 8,
        out_specs=HBM,
        scratch_shapes=[
            pltpu.VMEM((2, ROWS, GRID), f32),
            pltpu.VMEM((COLS, ROWS, 2 * LANES), f32),
            pltpu.VMEM((2, ROWS, GRID), f32),
            pltpu.SemaphoreType.DMA((GROUPS, 2)),
        ],
        compiler_params=PARAMS,
    )(scalars, chunks, t["fwd_y"], t["inv"], t["tw_y"], t["tw_x"], t["wavenum"], t["own"], t["step8"])


def solution(mesh):
    in_specs = (P(None, "gz", "wa", None), P("gz", "wa", None))
    out_specs = P(None, "gz", "wa", None)
    return jax.shard_map(
        on_device, mesh=mesh, in_specs=in_specs, out_specs=out_specs, check_vma=False
    )
```

```python
import math

import jax
import jax.numpy as jnp
import numpy as np
from jax import lax
from jax.experimental import pallas as pl
from jax.experimental.pallas import tpu as pltpu
from jax.sharding import PartitionSpec as P

time_step = 0.001
spacing = 1.0 / 32.0
rotation = 0.9
coupling = 400.0
z_coupling = 0.25

GRID = 2048
LANES = 128
COLS = 16
ROWS = 32
GROUPS = 4
PARTS_WA = 64

NEAR = (2.0 * z_coupling * z_coupling, z_coupling)
FAR = -0.5 * z_coupling * z_coupling
CENTRE = (1.0 - 3.0 * z_coupling * z_coupling, -2.0 * z_coupling)
CENTRE_EDGE = 1.0 - 2.5 * z_coupling * z_coupling


def tables():
    lane = np.arange(LANES)
    turned_lane = 32 * ((lane // 8) % 4) + 8 * (lane // 32) + lane % 8
    scale = 1.0 / math.sqrt(GRID)

    def matrices(order):
        angle = 2.0 * np.pi * ((order[:, None] * lane[None, :]) % LANES) / LANES
        cos, sin = np.cos(angle) * scale, np.sin(angle) * scale
        forward = np.block([[cos, -sin], [sin, cos]])
        return forward

    def split(matrix):
        high = matrix.astype(jnp.bfloat16)
        low = (matrix - high.astype(np.float64)).astype(jnp.bfloat16)
        return np.stack([np.asarray(high), np.asarray(low)])

    def twiddle(order):
        angle = 2.0 * np.pi * np.arange(COLS)[:, None] * order[None, :] / GRID
        return np.stack([np.cos(angle), np.sin(angle)]).astype(np.float32)

    angle = 2.0 * np.pi * ((lane[:, None] * lane[None, :]) % LANES) / LANES
    cos, sin = np.cos(angle) * scale, np.sin(angle) * scale
    backward = split(np.block([[cos, sin], [-sin, cos]]))
    mode = np.arange(COLS)[:, None] + COLS * lane[None, :]
    signed = np.where(mode < GRID // 2, mode, mode - GRID).astype(np.float64)
    wavenum = signed * (2.0 * np.pi / (GRID * spacing))
    slope = time_step * rotation * spacing * wavenum
    rows8 = slope[:, None, :] * np.arange(8)[None, :, None]
    own = np.stack([np.cos(rows8), np.sin(rows8)]).astype(np.float32)
    step8 = np.stack([np.cos(8.0 * slope), np.sin(8.0 * slope)]).astype(np.float32)
    return {
        "fwd_x": split(matrices(lane)),
        "fwd_y": split(matrices(turned_lane)),
        "inv": backward,
        "tw_x": twiddle(lane),
        "tw_y": twiddle(turned_lane),
        "wavenum": wavenum.astype(np.float32),
        "own": own,
        "step8": step8,
    }


def sincos(angle):
    turns = jnp.floor(angle * (2.0 / math.pi) + 0.5)
    rest = angle - turns * 1.5703125
    rest = rest - turns * 4.837512969970703e-4
    rest = rest - turns * 7.54978995489188e-8
    square = rest * rest
    sine = rest + rest * square * (
        -1.6666654611e-1 + square * (8.3321608736e-3 - square * 1.9515295891e-4)
    )
    cosine = 1.0 - 0.5 * square + square * square * (
        4.166664568298827e-2 + square * (-1.388731625493765e-3 + square * 2.443315711809948e-5)
    )
    quadrant = turns.astype(jnp.int32)
    swapped = (quadrant & 1) == 1
    sin_out = jnp.where(swapped, cosine, sine)
    cos_out = jnp.where(swapped, sine, cosine)
    sin_out = jnp.where((quadrant & 2) == 2, -sin_out, sin_out)
    cos_out = jnp.where(((quadrant + 1) & 2) == 2, -cos_out, cos_out)
    return sin_out, cos_out


def dft4(v, sign):
    (ar, ai), (br, bi), (cr, ci), (dr, di) = v
    sr, si, tr, ti = ar + cr, ai + ci, ar - cr, ai - ci
    ur, ui, wr, wi = br + dr, bi + di, br - dr, bi - di
    if sign > 0:
        p, q = (tr + wi, ti - wr), (tr - wi, ti + wr)
    else:
        p, q = (tr - wi, ti + wr), (tr + wi, ti - wr)
    return [(sr + ur, si + ui), p, (sr - ur, si - ui), q]


def turn16(v, power, sign):
    power %= 16
    re, im = v
    if power == 0:
        return v
    c, s = math.cos(2.0 * math.pi * power / 16), -sign * math.sin(2.0 * math.pi * power / 16)
    if power == 4:
        return (im, -re) if sign > 0 else (-im, re)
    if power % 2 == 0:
        h = math.sqrt(0.5)
        return (h * (_pm(re, c) + _pm(im, -s)), h * (_pm(re, s) + _pm(im, c)))
    return (re * c - im * s, re * s + im * c)


def _pm(x, sign):
    return x if sign > 0 else -x


def dft16(v, sign):
    low = [dft4([v[4 * a + b] for a in range(4)], sign) for b in range(4)]
    out = [None] * 16
    for k in range(4):
        high = dft4([turn16(low[b][k], b * k, sign) for b in range(4)], sign)
        for k2 in range(4):
            out[k + 4 * k2] = high[k2]
    return out


def swap_blocks(v):
    lane = lax.broadcasted_iota(jnp.int32, (8, LANES), 1)

    def stage(first, second, width):
        upper = (lane // width) % 2 == 1
        a = jnp.where(upper, pltpu.roll(second, width, 1), first)
        b = jnp.where(upper, second, pltpu.roll(first, LANES - width, 1))
        return a, b

    v0, v2 = stage(v[0], v[2], 64)
    v1, v3 = stage(v[1], v[3], 64)
    v0, v1 = stage(v0, v1, 32)
    v2, v3 = stage(v2, v3, 32)
    return [v0, v1, v2, v3]


def row_phases(first_row, wavenum, step8, sign):
    angle = time_step * (0.5 * wavenum * wavenum + (sign * rotation * first_row) * wavenum)
    sine, cosine = sincos(angle)
    re, im = cosine, -sine
    sr, si = step8[0], -sign * step8[1]
    out = [(re, im)]
    for _ in range(GROUPS - 1):
        re, im = re * sr - im * si, re * si + im * sr
        out.append((re, im))
    return out


def double_dot(left, table_ref):
    return jnp.dot(left, table_ref[0], preferred_element_type=jnp.float32) + jnp.dot(
        left, table_ref[1], preferred_element_type=jnp.float32
    )


def sweep(load, store, first_row, fwd_ref, inv_ref, tw_f_ref, tw_i_ref, wave_ref, own_ref, step_ref, buf, sign, finish=None):
    for g in range(GROUPS):
        rows = slice(8 * g, 8 * g + 8)
        out = dft16([load(g, c) for c in range(COLS)], 1)
        for m in range(COLS):
            re, im = out[m]
            if m > 0:
                c, s = tw_f_ref[0, m : m + 1, :], tw_f_ref[1, m : m + 1, :]
                re, im = re * c + im * s, im * c - re * s
            buf[m, rows, :LANES] = re
            buf[m, rows, LANES:] = im
    spectrum = double_dot(buf[...].reshape(COLS * ROWS, 2 * LANES).astype(jnp.bfloat16), fwd_ref)
    buf[...] = spectrum.reshape(COLS, ROWS, 2 * LANES)
    phases = row_phases(first_row, wave_ref[...], step_ref[...], sign)
    for m in range(COLS):
        own_re, own_im = own_ref[0, m], -sign * own_ref[1, m]
        for g in range(GROUPS):
            rows = slice(8 * g, 8 * g + 8)
            row_re, row_im = phases[g][0][m : m + 1, :], phases[g][1][m : m + 1, :]
            f_re, f_im = own_re * row_re - own_im * row_im, own_re * row_im + own_im * row_re
            re, im = buf[m, rows, :LANES], buf[m, rows, LANES:]
            buf[m, rows, :LANES] = re * f_re - im * f_im
            buf[m, rows, LANES:] = re * f_im + im * f_re
    turned = double_dot(buf[...].reshape(COLS * ROWS, 2 * LANES).astype(jnp.bfloat16), inv_ref)
    buf[...] = turned.reshape(COLS, ROWS, 2 * LANES)
    for g in range(GROUPS):
        rows = slice(8 * g, 8 * g + 8)
        terms = []
        for m in range(COLS):
            re, im = buf[m, rows, :LANES], buf[m, rows, LANES:]
            if m > 0:
                c, s = tw_i_ref[0, m : m + 1, :], tw_i_ref[1, m : m + 1, :]
                re, im = re * c - im * s, im * c + re * s
            terms.append((re, im))
        for c, (re, im) in enumerate(dft16(terms, -1)):
            store(g, c, re, im)
        if finish is not None:
            finish(g)


def potential_kernel(wave_hbm, potential_hbm, out_ref, wave_ref, potential_ref, sems):
    half = GRID // 2
    blocks = [(slice(16 * g, 16 * g + 16), slice(half * h, half * h + half)) for g in range(2) for h in range(2)]
    copies = []
    for b, (rows, at) in enumerate(blocks):
        copies.append([
            pltpu.make_async_copy(wave_hbm.at[0, 0, rows, at], wave_ref.at[0, rows, at], sems.at[b, 0]),
            pltpu.make_async_copy(wave_hbm.at[1, 0, rows, at], wave_ref.at[1, rows, at], sems.at[b, 1]),
            pltpu.make_async_copy(potential_hbm.at[0, rows, at], potential_ref.at[rows, at], sems.at[b, 2]),
        ])
        for copy in copies[-1]:
            copy.start()
    for (rows, at), waits in zip(blocks, copies):
        for copy in waits:
            copy.wait()
        for first in range(at.start, at.stop, LANES):
            cols = slice(first, first + LANES)
            re, im, pot = wave_ref[0, rows, cols], wave_ref[1, rows, cols], potential_ref[rows, cols]
            sine, cosine = sincos(time_step * (pot + coupling * (re * re + im * im)))
            out_ref[0, rows, cols] = (re * cosine + im * sine).astype(jnp.bfloat16)
            out_ref[1, rows, cols] = (im * cosine - re * sine).astype(jnp.bfloat16)


def message_kernel(own_ref, far_ref, out_ref):
    for p in range(2):
        total = own_ref[p].astype(jnp.float32) + far_ref[p].astype(jnp.float32)
        out_ref[p] = total.astype(jnp.bfloat16)


def x_kernel(scalar_ref, own_ref, near_ref, far_ref, across_ref, fwd_ref, inv_ref, tw_ref, wave_ref, rows_ref, step_ref, out_ref, mixed, buf, swept):
    centre = scalar_ref[1]
    for g in range(2):
        rows = slice(16 * g, 16 * g + 16)
        for c in range(COLS):
            at = slice(LANES * c, LANES * c + LANES)
            re, im, nre, nim, fre, fim, are, aim = (
                ref[p, rows, at].astype(jnp.float32)
                for ref in (own_ref, near_ref, far_ref, across_ref)
                for p in range(2)
            )
            mixed[0, rows, at] = centre * re - CENTRE[1] * im + (NEAR[0] * nre - NEAR[1] * nim) + FAR * (fre + are)
            mixed[1, rows, at] = centre * im + CENTRE[1] * re + (NEAR[0] * nim + NEAR[1] * nre) + FAR * (fim + aim)

    def load(g, c):
        at = slice(LANES * c, LANES * c + LANES)
        return mixed[0, 8 * g : 8 * g + 8, at], mixed[1, 8 * g : 8 * g + 8, at]

    def store(g, c, re, im):
        swept[c, 0, g] = re
        swept[c, 1, g] = im

    sweep(load, store, scalar_ref[0], fwd_ref, inv_ref, tw_ref, tw_ref, wave_ref, rows_ref, step_ref, buf, 1.0)
    for c in range(COLS):
        re = swap_blocks([swept[c, 0, g] for g in range(GROUPS)])
        im = swap_blocks([swept[c, 1, g] for g in range(GROUPS)])
        for q in range(4):
            out_ref[4 * c + q] = jnp.concatenate([re[q], im[q]], axis=0).astype(jnp.bfloat16)


def y_kernel(scalar_ref, in_ref, fwd_ref, inv_ref, tw_f_ref, tw_i_ref, wave_ref, rows_ref, step_ref, out_hbm, field, buf, out_ref, sems):
    for s in range(4):
        block = in_ref[16 * s : 16 * s + 16].astype(jnp.float32)
        for p in range(2):
            flipped = jnp.transpose(block[:, 8 * p : 8 * p + 8, :].reshape(LANES, LANES))
            for x in range(4):
                parts = swap_blocks([flipped[32 * g + 8 * x : 32 * g + 8 * x + 8] for g in range(4)])
                for a in range(4):
                    field[p, 8 * x : 8 * x + 8, LANES * (4 * s + a) : LANES * (4 * s + a + 1)] = parts[a]

    def load(g, c):
        at = slice(LANES * c, LANES * c + LANES)
        return field[0, 8 * g : 8 * g + 8, at], field[1, 8 * g : 8 * g + 8, at]

    def store(g, c, re, im):
        at = slice(LANES * c, LANES * c + LANES)
        out_ref[0, 8 * g : 8 * g + 8, at] = re
        out_ref[1, 8 * g : 8 * g + 8, at] = im

    copies = []

    def send(g):
        rows = slice(8 * g, 8 * g + 8)
        for p in range(2):
            copies.append(pltpu.make_async_copy(out_ref.at[p, rows], out_hbm.at[p, 0, rows], sems.at[g, p]))
            copies[-1].start()

    sweep(load, store, scalar_ref[0], fwd_ref, inv_ref, tw_f_ref, tw_i_ref, wave_ref, rows_ref, step_ref, buf, -1.0, send)
    for copy in copies:
        copy.wait()


SMEM = pl.BlockSpec(memory_space=pltpu.SMEM)
HBM = pl.BlockSpec(memory_space=pltpu.HBM)
VMEM = pl.BlockSpec(memory_space=pltpu.VMEM)
PARAMS = pltpu.CompilerParams(vmem_limit_bytes=48 * 1024 * 1024)


def on_device(wave, potential):
    t = tables()
    f32, bf16 = jnp.float32, jnp.bfloat16
    row_base = lax.axis_index("wa") * ROWS - GRID // 2
    plane = lax.axis_index("gz")
    edge = (plane == 0) | (plane == 7)
    scalars = jnp.stack([row_base.astype(f32) * spacing, jnp.where(edge, CENTRE_EDGE, CENTRE[0])])
    own = pl.pallas_call(
        potential_kernel,
        out_shape=jax.ShapeDtypeStruct((2, ROWS, GRID), bf16),
        in_specs=[HBM, HBM],
        out_specs=VMEM,
        scratch_shapes=[
            pltpu.VMEM((2, ROWS, GRID), f32),
            pltpu.VMEM((ROWS, GRID), f32),
            pltpu.SemaphoreType.DMA((4, 3)),
        ],
        compiler_params=PARAMS,
    )(pltpu.with_memory_space_constraint(wave, pltpu.HBM), pltpu.with_memory_space_constraint(potential, pltpu.HBM))
    outward = [(i, i - 2) for i in (2, 4, 6)] + [(i, i + 2) for i in (1, 3, 5)]
    inward = [(i, i + 2) for i in (0, 2, 4)] + [(i, i - 2) for i in (3, 5, 7)]
    far = lax.ppermute(own, "gz", outward)
    across = lax.ppermute(own, "gz", inward)
    message = pl.pallas_call(
        message_kernel,
        out_shape=jax.ShapeDtypeStruct((2, ROWS, GRID), bf16),
        in_specs=[VMEM, VMEM],
        out_specs=VMEM,
        compiler_params=PARAMS,
    )(own, far)
    near = lax.ppermute(message, "gz", [(i, i ^ 1) for i in range(8)])
    chunks = pl.pallas_call(
        x_kernel,
        out_shape=jax.ShapeDtypeStruct((PARTS_WA, 16, LANES), bf16),
        in_specs=[SMEM] + [VMEM] * 10,
        out_specs=VMEM,
        scratch_shapes=[
            pltpu.VMEM((2, ROWS, GRID), f32),
            pltpu.VMEM((COLS, ROWS, 2 * LANES), f32),
            pltpu.VMEM((COLS, 2, GROUPS, 8, LANES), f32),
        ],
        compiler_params=PARAMS,
    )(scalars, own, near, far, across, t["fwd_x"], t["inv"], t["tw_x"], t["wavenum"], t["own"], t["step8"])
    chunks = lax.all_to_all(chunks, "wa", 0, 0, tiled=True)
    return pl.pallas_call(
        y_kernel,
        out_shape=jax.ShapeDtypeStruct((2, 1, ROWS, GRID), f32),
        in_specs=[SMEM] + [VMEM] * 8,
        out_specs=HBM,
        scratch_shapes=[
            pltpu.VMEM((2, ROWS, GRID), f32),
            pltpu.VMEM((COLS, ROWS, 2 * LANES), f32),
            pltpu.VMEM((2, ROWS, GRID), f32),
            pltpu.SemaphoreType.DMA((GROUPS, 2)),
        ],
        compiler_params=PARAMS,
    )(scalars, chunks, t["fwd_y"], t["inv"], t["tw_y"], t["tw_x"], t["wavenum"], t["own"], t["step8"])


def solution(mesh):
    in_specs = (P(None, "gz", "wa", None), P("gz", "wa", None))
    out_specs = P(None, "gz", "wa", None)
    return jax.shard_map(
        on_device, mesh=mesh, in_specs=in_specs, out_specs=out_specs, check_vma=False
    )
```

```python
import math

import jax
import jax.numpy as jnp
import numpy as np
from jax import lax
from jax.experimental import pallas as pl
from jax.experimental.pallas import tpu as pltpu
from jax.sharding import PartitionSpec as P

time_step = 0.001
spacing = 1.0 / 32.0
rotation = 0.9
coupling = 400.0
z_coupling = 0.25

GRID = 2048
LANES = 128
COLS = 16
ROWS = 32
GROUPS = 4
PARTS_WA = 64

NEAR = (2.0 * z_coupling * z_coupling, z_coupling)
FAR = -0.5 * z_coupling * z_coupling
CENTRE = (1.0 - 3.0 * z_coupling * z_coupling, -2.0 * z_coupling)
CENTRE_EDGE = 1.0 - 2.5 * z_coupling * z_coupling


def tables():
    lane = np.arange(LANES)
    turned_lane = 32 * ((lane // 8) % 4) + 8 * (lane // 32) + lane % 8
    scale = 1.0 / math.sqrt(GRID)

    def matrices(order):
        angle = 2.0 * np.pi * ((order[:, None] * lane[None, :]) % LANES) / LANES
        cos, sin = np.cos(angle) * scale, np.sin(angle) * scale
        forward = np.block([[cos, -sin], [sin, cos]])
        return forward

    def split(matrix):
        high = matrix.astype(jnp.bfloat16)
        low = (matrix - high.astype(np.float64)).astype(jnp.bfloat16)
        return np.concatenate([np.asarray(high), np.asarray(low)])

    def twiddle(order):
        angle = 2.0 * np.pi * np.arange(COLS)[:, None] * order[None, :] / GRID
        return np.stack([np.cos(angle), np.sin(angle)]).astype(np.float32)

    angle = 2.0 * np.pi * ((lane[:, None] * lane[None, :]) % LANES) / LANES
    cos, sin = np.cos(angle) * scale, np.sin(angle) * scale
    backward = split(np.block([[cos, sin], [-sin, cos]]))
    mode = np.arange(COLS)[:, None] + COLS * lane[None, :]
    signed = np.where(mode < GRID // 2, mode, mode - GRID).astype(np.float64)
    wavenum = signed * (2.0 * np.pi / (GRID * spacing))
    slope = time_step * rotation * spacing * wavenum
    rows8 = slope[:, None, :] * np.arange(8)[None, :, None]
    own = np.stack([np.cos(rows8), np.sin(rows8)]).astype(np.float32)
    step8 = np.stack([np.cos(8.0 * slope), np.sin(8.0 * slope)]).astype(np.float32)
    return {
        "fwd_x": split(matrices(lane)),
        "fwd_y": split(matrices(turned_lane)),
        "inv": backward,
        "tw_x": twiddle(lane),
        "tw_y": twiddle(turned_lane),
        "wavenum": wavenum.astype(np.float32),
        "own": own,
        "step8": step8,
    }


def sincos(angle):
    turns = jnp.floor(angle * (2.0 / math.pi) + 0.5)
    rest = angle - turns * 1.5703125
    rest = rest - turns * 4.837512969970703e-4
    rest = rest - turns * 7.54978995489188e-8
    square = rest * rest
    sine = rest + rest * square * (
        -1.6666654611e-1 + square * (8.3321608736e-3 - square * 1.9515295891e-4)
    )
    cosine = 1.0 - 0.5 * square + square * square * (
        4.166664568298827e-2 + square * (-1.388731625493765e-3 + square * 2.443315711809948e-5)
    )
    quadrant = turns.astype(jnp.int32)
    swapped = (quadrant & 1) == 1
    sin_out = jnp.where(swapped, cosine, sine)
    cos_out = jnp.where(swapped, sine, cosine)
    sin_out = jnp.where((quadrant & 2) == 2, -sin_out, sin_out)
    cos_out = jnp.where(((quadrant + 1) & 2) == 2, -cos_out, cos_out)
    return sin_out, cos_out


def dft4(v, sign):
    (ar, ai), (br, bi), (cr, ci), (dr, di) = v
    sr, si, tr, ti = ar + cr, ai + ci, ar - cr, ai - ci
    ur, ui, wr, wi = br + dr, bi + di, br - dr, bi - di
    if sign > 0:
        p, q = (tr + wi, ti - wr), (tr - wi, ti + wr)
    else:
        p, q = (tr - wi, ti + wr), (tr + wi, ti - wr)
    return [(sr + ur, si + ui), p, (sr - ur, si - ui), q]


def turn16(v, power, sign):
    power %= 16
    re, im = v
    if power == 0:
        return v
    c, s = math.cos(2.0 * math.pi * power / 16), -sign * math.sin(2.0 * math.pi * power / 16)
    if power == 4:
        return (im, -re) if sign > 0 else (-im, re)
    if power % 2 == 0:
        h = math.sqrt(0.5)
        return (h * (_pm(re, c) + _pm(im, -s)), h * (_pm(re, s) + _pm(im, c)))
    return (re * c - im * s, re * s + im * c)


def _pm(x, sign):
    return x if sign > 0 else -x


def dft16(v, sign):
    low = [dft4([v[4 * a + b] for a in range(4)], sign) for b in range(4)]
    out = [None] * 16
    for k in range(4):
        high = dft4([turn16(low[b][k], b * k, sign) for b in range(4)], sign)
        for k2 in range(4):
            out[k + 4 * k2] = high[k2]
    return out


def swap_blocks(v):
    lane = lax.broadcasted_iota(jnp.int32, (8, LANES), 1)

    def stage(first, second, width):
        upper = (lane // width) % 2 == 1
        a = jnp.where(upper, pltpu.roll(second, width, 1), first)
        b = jnp.where(upper, second, pltpu.roll(first, LANES - width, 1))
        return a, b

    v0, v2 = stage(v[0], v[2], 64)
    v1, v3 = stage(v[1], v[3], 64)
    v0, v1 = stage(v0, v1, 32)
    v2, v3 = stage(v2, v3, 32)
    return [v0, v1, v2, v3]


def row_phases(first_row, wavenum, step8, sign):
    angle = time_step * (0.5 * wavenum * wavenum + (sign * rotation * first_row) * wavenum)
    sine, cosine = sincos(angle)
    re, im = cosine, -sine
    sr, si = step8[0], -sign * step8[1]
    out = [(re, im)]
    for _ in range(GROUPS - 1):
        re, im = re * sr - im * si, re * si + im * sr
        out.append((re, im))
    return out


def matrix_stage(re, im, table_ref):
    left = jnp.concatenate(
        [
            jnp.concatenate([jnp.concatenate([part[g][m] for g in range(GROUPS)], axis=0) for part in (re, im)], axis=1)
            for m in range(COLS)
        ],
        axis=0,
    ).astype(jnp.bfloat16)
    left = jnp.concatenate([left, left], axis=1)
    return jnp.dot(left, table_ref[...], preferred_element_type=jnp.float32)


def sweep(load, store, first_row, fwd_ref, inv_ref, tw_f_ref, tw_i_ref, wave_ref, rows_ref, step_ref, sign, finish=None):
    def parts_of(value, m, g):
        rows = slice(ROWS * m + 8 * g, ROWS * m + 8 * g + 8)
        return value[rows, :LANES], value[rows, LANES:]

    re_in, im_in = [], []
    for g in range(GROUPS):
        out = dft16([load(g, c) for c in range(COLS)], 1)
        for m in range(1, COLS):
            re, im = out[m]
            c, s = tw_f_ref[0, m : m + 1, :], tw_f_ref[1, m : m + 1, :]
            out[m] = (re * c + im * s, im * c - re * s)
        re_in.append([v[0] for v in out])
        im_in.append([v[1] for v in out])
    spectrum = matrix_stage(re_in, im_in, fwd_ref)
    phases = row_phases(first_row, wave_ref[...], step_ref[...], sign)
    re_in, im_in = [[None] * COLS for _ in range(GROUPS)], [[None] * COLS for _ in range(GROUPS)]
    for m in range(COLS):
        own_re, own_im = rows_ref[0, m], -sign * rows_ref[1, m]
        for g in range(GROUPS):
            row_re, row_im = phases[g][0][m : m + 1, :], phases[g][1][m : m + 1, :]
            f_re, f_im = own_re * row_re - own_im * row_im, own_re * row_im + own_im * row_re
            re, im = parts_of(spectrum, m, g)
            re_in[g][m], im_in[g][m] = re * f_re - im * f_im, re * f_im + im * f_re
    turned = matrix_stage(re_in, im_in, inv_ref)
    for g in range(GROUPS):
        terms = []
        for m in range(COLS):
            re, im = parts_of(turned, m, g)
            if m > 0:
                c, s = tw_i_ref[0, m : m + 1, :], tw_i_ref[1, m : m + 1, :]
                re, im = re * c - im * s, im * c + re * s
            terms.append((re, im))
        for c, (re, im) in enumerate(dft16(terms, -1)):
            store(g, c, re, im)
        if finish is not None:
            finish(g)


def potential_kernel(wave_hbm, potential_hbm, out_ref, wave_ref, potential_ref, sems):
    half = GRID // 2
    blocks = [(slice(16 * g, 16 * g + 16), slice(half * h, half * h + half)) for g in range(2) for h in range(2)]
    copies = []
    for b, (rows, at) in enumerate(blocks):
        copies.append([
            pltpu.make_async_copy(wave_hbm.at[0, 0, rows, at], wave_ref.at[0, rows, at], sems.at[b, 0]),
            pltpu.make_async_copy(wave_hbm.at[1, 0, rows, at], wave_ref.at[1, rows, at], sems.at[b, 1]),
            pltpu.make_async_copy(potential_hbm.at[0, rows, at], potential_ref.at[rows, at], sems.at[b, 2]),
        ])
        for copy in copies[-1]:
            copy.start()
    for (rows, at), waits in zip(blocks, copies):
        for copy in waits:
            copy.wait()
        for first in range(at.start, at.stop, LANES):
            cols = slice(first, first + LANES)
            re, im, pot = wave_ref[0, rows, cols], wave_ref[1, rows, cols], potential_ref[rows, cols]
            sine, cosine = sincos(time_step * (pot + coupling * (re * re + im * im)))
            out_ref[0, rows, cols] = (re * cosine + im * sine).astype(jnp.bfloat16)
            out_ref[1, rows, cols] = (im * cosine - re * sine).astype(jnp.bfloat16)


def message_kernel(own_ref, beside_ref, out_ref):
    re, im = own_ref[0].astype(jnp.float32), own_ref[1].astype(jnp.float32)
    bre, bim = beside_ref[0].astype(jnp.float32), beside_ref[1].astype(jnp.float32)
    out_ref[0] = (NEAR[0] * re - NEAR[1] * im + FAR * bre).astype(jnp.bfloat16)
    out_ref[1] = (NEAR[0] * im + NEAR[1] * re + FAR * bim).astype(jnp.bfloat16)


def x_kernel(scalar_ref, own_ref, beside_ref, near_ref, across_ref, fwd_ref, inv_ref, tw_ref, wave_ref, rows_ref, step_ref, out_ref, mixed, swept):
    centre = scalar_ref[1]
    for g in range(2):
        rows = slice(16 * g, 16 * g + 16)
        for c in range(COLS):
            at = slice(LANES * c, LANES * c + LANES)
            re, im, bre, bim, nre, nim, are, aim = (
                ref[p, rows, at].astype(jnp.float32)
                for ref in (own_ref, beside_ref, near_ref, across_ref)
                for p in range(2)
            )
            mixed[0, rows, at] = centre * re - CENTRE[1] * im + (NEAR[0] * bre - NEAR[1] * bim) + (nre + FAR * are)
            mixed[1, rows, at] = centre * im + CENTRE[1] * re + (NEAR[0] * bim + NEAR[1] * bre) + (nim + FAR * aim)

    def load(g, c):
        at = slice(LANES * c, LANES * c + LANES)
        return mixed[0, 8 * g : 8 * g + 8, at], mixed[1, 8 * g : 8 * g + 8, at]

    def store(g, c, re, im):
        swept[c, 0, g] = re
        swept[c, 1, g] = im

    sweep(load, store, scalar_ref[0], fwd_ref, inv_ref, tw_ref, tw_ref, wave_ref, rows_ref, step_ref, 1.0)
    for c in range(COLS):
        re = swap_blocks([swept[c, 0, g] for g in range(GROUPS)])
        im = swap_blocks([swept[c, 1, g] for g in range(GROUPS)])
        for q in range(4):
            out_ref[4 * c + q] = jnp.concatenate([re[q], im[q]], axis=0).astype(jnp.bfloat16)


def y_kernel(scalar_ref, in_ref, fwd_ref, inv_ref, tw_f_ref, tw_i_ref, wave_ref, rows_ref, step_ref, out_hbm, field, out_ref, sems):
    for s in range(4):
        block = in_ref[16 * s : 16 * s + 16].astype(jnp.float32)
        for p in range(2):
            flipped = jnp.transpose(block[:, 8 * p : 8 * p + 8, :].reshape(LANES, LANES))
            for x in range(4):
                parts = swap_blocks([flipped[32 * g + 8 * x : 32 * g + 8 * x + 8] for g in range(4)])
                for a in range(4):
                    field[p, 8 * x : 8 * x + 8, LANES * (4 * s + a) : LANES * (4 * s + a + 1)] = parts[a]

    def load(g, c):
        at = slice(LANES * c, LANES * c + LANES)
        return field[0, 8 * g : 8 * g + 8, at], field[1, 8 * g : 8 * g + 8, at]

    def store(g, c, re, im):
        at = slice(LANES * c, LANES * c + LANES)
        out_ref[0, 8 * g : 8 * g + 8, at] = re
        out_ref[1, 8 * g : 8 * g + 8, at] = im

    copies = []

    def send(g):
        rows = slice(8 * g, 8 * g + 8)
        for p in range(2):
            copies.append(pltpu.make_async_copy(out_ref.at[p, rows], out_hbm.at[p, 0, rows], sems.at[g, p]))
            copies[-1].start()

    sweep(load, store, scalar_ref[0], fwd_ref, inv_ref, tw_f_ref, tw_i_ref, wave_ref, rows_ref, step_ref, -1.0, send)
    for copy in copies:
        copy.wait()


SMEM = pl.BlockSpec(memory_space=pltpu.SMEM)
HBM = pl.BlockSpec(memory_space=pltpu.HBM)
VMEM = pl.BlockSpec(memory_space=pltpu.VMEM)
PARAMS = pltpu.CompilerParams(vmem_limit_bytes=48 * 1024 * 1024)


def on_device(wave, potential):
    t = tables()
    f32, bf16 = jnp.float32, jnp.bfloat16
    row_base = lax.axis_index("wa") * ROWS - GRID // 2
    plane = lax.axis_index("gz")
    edge = (plane == 0) | (plane == 7)
    scalars = jnp.stack([row_base.astype(f32) * spacing, jnp.where(edge, CENTRE_EDGE, CENTRE[0])])
    own = pl.pallas_call(
        potential_kernel,
        out_shape=jax.ShapeDtypeStruct((2, ROWS, GRID), bf16),
        in_specs=[HBM, HBM],
        out_specs=VMEM,
        scratch_shapes=[
            pltpu.VMEM((2, ROWS, GRID), f32),
            pltpu.VMEM((ROWS, GRID), f32),
            pltpu.SemaphoreType.DMA((4, 3)),
        ],
        compiler_params=PARAMS,
    )(pltpu.with_memory_space_constraint(wave, pltpu.HBM), pltpu.with_memory_space_constraint(potential, pltpu.HBM))
    outward = [(i, i - 1) for i in (2, 4, 6)] + [(i, i + 1) for i in (1, 3, 5)]
    inward = [(i, i + 2) for i in (0, 2, 4)] + [(i, i - 2) for i in (3, 5, 7)]
    beside = lax.ppermute(own, "gz", outward)
    across = lax.ppermute(own, "gz", inward)
    message = pl.pallas_call(
        message_kernel,
        out_shape=jax.ShapeDtypeStruct((2, ROWS, GRID), bf16),
        in_specs=[VMEM, VMEM],
        out_specs=VMEM,
        compiler_params=PARAMS,
    )(own, beside)
    near = lax.ppermute(message, "gz", [(i, i ^ 1) for i in range(8)])
    chunks = pl.pallas_call(
        x_kernel,
        out_shape=jax.ShapeDtypeStruct((PARTS_WA, 16, LANES), bf16),
        in_specs=[SMEM] + [VMEM] * 10,
        out_specs=VMEM,
        scratch_shapes=[
            pltpu.VMEM((2, ROWS, GRID), f32),
            pltpu.VMEM((COLS, 2, GROUPS, 8, LANES), f32),
        ],
        compiler_params=PARAMS,
    )(scalars, own, beside, near, across, t["fwd_x"], t["inv"], t["tw_x"], t["wavenum"], t["own"], t["step8"])
    chunks = lax.all_to_all(chunks, "wa", 0, 0, tiled=True)
    return pl.pallas_call(
        y_kernel,
        out_shape=jax.ShapeDtypeStruct((2, 1, ROWS, GRID), f32),
        in_specs=[SMEM] + [VMEM] * 8,
        out_specs=HBM,
        scratch_shapes=[
            pltpu.VMEM((2, ROWS, GRID), f32),
            pltpu.VMEM((2, ROWS, GRID), f32),
            pltpu.SemaphoreType.DMA((GROUPS, 2)),
        ],
        compiler_params=PARAMS,
    )(scalars, chunks, t["fwd_y"], t["inv"], t["tw_y"], t["tw_x"], t["wavenum"], t["own"], t["step8"])


def solution(mesh):
    in_specs = (P(None, "gz", "wa", None), P("gz", "wa", None))
    out_specs = P(None, "gz", "wa", None)
    return jax.shard_map(
        on_device, mesh=mesh, in_specs=in_specs, out_specs=out_specs, check_vma=False
    )
```

```python
import math

import jax
import jax.numpy as jnp
import numpy as np
from jax import lax
from jax.experimental import pallas as pl
from jax.experimental.pallas import tpu as pltpu
from jax.sharding import PartitionSpec as P

time_step = 0.001
spacing = 1.0 / 32.0
rotation = 0.9
coupling = 400.0
z_coupling = 0.25

GRID = 2048
LANES = 128
COLS = 16
ROWS = 32
GROUPS = 4
PARTS_WA = 64

NEAR = (2.0 * z_coupling * z_coupling, z_coupling)
FAR = -0.5 * z_coupling * z_coupling
CENTRE = (1.0 - 3.0 * z_coupling * z_coupling, -2.0 * z_coupling)
CENTRE_EDGE = 1.0 - 2.5 * z_coupling * z_coupling


def tables():
    lane = np.arange(LANES)
    turned_lane = 32 * ((lane // 8) % 4) + 8 * (lane // 32) + lane % 8
    scale = 1.0 / math.sqrt(GRID)

    def matrices(order):
        angle = 2.0 * np.pi * ((order[:, None] * lane[None, :]) % LANES) / LANES
        cos, sin = np.cos(angle) * scale, np.sin(angle) * scale
        forward = np.block([[cos, -sin], [sin, cos]])
        return forward

    def split(matrix):
        high = matrix.astype(jnp.bfloat16)
        low = (matrix - high.astype(np.float64)).astype(jnp.bfloat16)
        return np.concatenate([np.asarray(high), np.asarray(low)])

    def twiddle(order):
        angle = 2.0 * np.pi * np.arange(COLS)[:, None] * order[None, :] / GRID
        return np.stack([np.cos(angle), np.sin(angle)]).astype(np.float32)

    angle = 2.0 * np.pi * ((lane[:, None] * lane[None, :]) % LANES) / LANES
    cos, sin = np.cos(angle) * scale, np.sin(angle) * scale
    backward = split(np.block([[cos, sin], [-sin, cos]]))
    mode = np.arange(COLS)[:, None] + COLS * lane[None, :]
    signed = np.where(mode < GRID // 2, mode, mode - GRID).astype(np.float64)
    wavenum = signed * (2.0 * np.pi / (GRID * spacing))
    slope = time_step * rotation * spacing * wavenum
    rows8 = slope[:, None, :] * np.arange(8)[None, :, None]
    own = np.stack([np.cos(rows8), np.sin(rows8)]).astype(np.float32)
    step8 = np.stack([np.cos(8.0 * slope), np.sin(8.0 * slope)]).astype(np.float32)
    return {
        "fwd_x": split(matrices(lane)),
        "fwd_y": split(matrices(turned_lane)),
        "inv": backward,
        "tw_x": twiddle(lane),
        "tw_y": twiddle(turned_lane),
        "wavenum": wavenum.astype(np.float32),
        "own": own,
        "step8": step8,
    }


SINE = (6.283182621002197, -41.34142303466797, 81.59618377685547, -76.5801010131836, 41.205387115478516, -12.271249771118164)
COSINE = (0.9999992251396179, -19.738983154296875, 64.92872619628906, -85.27239227294922, 58.794029235839844, -21.076766967773438)


def sincos(angle):
    turns = angle * (0.5 / math.pi)
    rest = turns - jnp.floor(turns + 0.5)
    square = rest * rest
    sine, cosine = SINE[-1], COSINE[-1]
    for first, second in zip(SINE[-2::-1], COSINE[-2::-1]):
        sine = sine * square + first
        cosine = cosine * square + second
    return sine * rest, cosine


def dft4(v, sign):
    (ar, ai), (br, bi), (cr, ci), (dr, di) = v
    sr, si, tr, ti = ar + cr, ai + ci, ar - cr, ai - ci
    ur, ui, wr, wi = br + dr, bi + di, br - dr, bi - di
    if sign > 0:
        p, q = (tr + wi, ti - wr), (tr - wi, ti + wr)
    else:
        p, q = (tr - wi, ti + wr), (tr + wi, ti - wr)
    return [(sr + ur, si + ui), p, (sr - ur, si - ui), q]


def turn16(v, power, sign):
    power %= 16
    re, im = v
    if power == 0:
        return v
    c, s = math.cos(2.0 * math.pi * power / 16), -sign * math.sin(2.0 * math.pi * power / 16)
    if power == 4:
        return (im, -re) if sign > 0 else (-im, re)
    if power % 2 == 0:
        h = math.sqrt(0.5)
        return (h * (_pm(re, c) + _pm(im, -s)), h * (_pm(re, s) + _pm(im, c)))
    return (re * c - im * s, re * s + im * c)


def _pm(x, sign):
    return x if sign > 0 else -x


def dft16(v, sign):
    low = [dft4([v[4 * a + b] for a in range(4)], sign) for b in range(4)]
    out = [None] * 16
    for k in range(4):
        high = dft4([turn16(low[b][k], b * k, sign) for b in range(4)], sign)
        for k2 in range(4):
            out[k + 4 * k2] = high[k2]
    return out


def swap_blocks(v):
    lane = lax.broadcasted_iota(jnp.int32, (8, LANES), 1)

    def stage(first, second, width):
        upper = (lane // width) % 2 == 1
        a = jnp.where(upper, pltpu.roll(second, width, 1), first)
        b = jnp.where(upper, second, pltpu.roll(first, LANES - width, 1))
        return a, b

    v0, v2 = stage(v[0], v[2], 64)
    v1, v3 = stage(v[1], v[3], 64)
    v0, v1 = stage(v0, v1, 32)
    v2, v3 = stage(v2, v3, 32)
    return [v0, v1, v2, v3]


def row_phases(first_row, wavenum, step8, sign):
    angle = time_step * (0.5 * wavenum * wavenum + (sign * rotation * first_row) * wavenum)
    sine, cosine = sincos(angle)
    re, im = cosine, -sine
    sr, si = step8[0], -sign * step8[1]
    out = [(re, im)]
    for _ in range(GROUPS - 1):
        re, im = re * sr - im * si, re * si + im * sr
        out.append((re, im))
    return out


def matrix_stage(re, im, table_ref):
    left = jnp.concatenate(
        [
            jnp.concatenate([jnp.concatenate([part[g][m] for g in range(GROUPS)], axis=0) for part in (re, im)], axis=1)
            for m in range(COLS)
        ],
        axis=0,
    ).astype(jnp.bfloat16)
    left = jnp.concatenate([left, left], axis=1)
    return jnp.dot(left, table_ref[...], preferred_element_type=jnp.float32)


def sweep(load, store, first_row, fwd_ref, inv_ref, tw_f_ref, tw_i_ref, wave_ref, rows_ref, step_ref, sign, finish=None):
    def parts_of(value, m, g):
        rows = slice(ROWS * m + 8 * g, ROWS * m + 8 * g + 8)
        return value[rows, :LANES], value[rows, LANES:]

    re_in, im_in = [], []
    for g in range(GROUPS):
        out = dft16([load(g, c) for c in range(COLS)], 1)
        for m in range(1, COLS):
            re, im = out[m]
            c, s = tw_f_ref[0, m : m + 1, :], tw_f_ref[1, m : m + 1, :]
            out[m] = (re * c + im * s, im * c - re * s)
        re_in.append([v[0] for v in out])
        im_in.append([v[1] for v in out])
    spectrum = matrix_stage(re_in, im_in, fwd_ref)
    phases = row_phases(first_row, wave_ref[...], step_ref[...], sign)
    re_in, im_in = [[None] * COLS for _ in range(GROUPS)], [[None] * COLS for _ in range(GROUPS)]
    for m in range(COLS):
        own_re, own_im = rows_ref[0, m], -sign * rows_ref[1, m]
        for g in range(GROUPS):
            row_re, row_im = phases[g][0][m : m + 1, :], phases[g][1][m : m + 1, :]
            f_re, f_im = own_re * row_re - own_im * row_im, own_re * row_im + own_im * row_re
            re, im = parts_of(spectrum, m, g)
            re_in[g][m], im_in[g][m] = re * f_re - im * f_im, re * f_im + im * f_re
    turned = matrix_stage(re_in, im_in, inv_ref)
    for g in range(GROUPS):
        terms = []
        for m in range(COLS):
            re, im = parts_of(turned, m, g)
            if m > 0:
                c, s = tw_i_ref[0, m : m + 1, :], tw_i_ref[1, m : m + 1, :]
                re, im = re * c - im * s, im * c + re * s
            terms.append((re, im))
        for c, (re, im) in enumerate(dft16(terms, -1)):
            store(g, c, re, im)
        if finish is not None:
            finish(g)


def potential_kernel(wave_hbm, potential_hbm, out_ref, wave_ref, potential_ref, sems):
    half = GRID // 2
    blocks = [(slice(16 * g, 16 * g + 16), slice(half * h, half * h + half)) for g in range(2) for h in range(2)]
    copies = []
    for b, (rows, at) in enumerate(blocks):
        copies.append([
            pltpu.make_async_copy(wave_hbm.at[0, 0, rows, at], wave_ref.at[0, rows, at], sems.at[b, 0]),
            pltpu.make_async_copy(wave_hbm.at[1, 0, rows, at], wave_ref.at[1, rows, at], sems.at[b, 1]),
            pltpu.make_async_copy(potential_hbm.at[0, rows, at], potential_ref.at[rows, at], sems.at[b, 2]),
        ])
        for copy in copies[-1]:
            copy.start()
    for (rows, at), waits in zip(blocks, copies):
        for copy in waits:
            copy.wait()
        for first in range(at.start, at.stop, LANES):
            cols = slice(first, first + LANES)
            re, im, pot = wave_ref[0, rows, cols], wave_ref[1, rows, cols], potential_ref[rows, cols]
            sine, cosine = sincos(time_step * (pot + coupling * (re * re + im * im)))
            out_ref[0, rows, cols] = (re * cosine + im * sine).astype(jnp.bfloat16)
            out_ref[1, rows, cols] = (im * cosine - re * sine).astype(jnp.bfloat16)


def message_kernel(own_ref, beside_ref, out_ref):
    re, im = own_ref[0].astype(jnp.float32), own_ref[1].astype(jnp.float32)
    bre, bim = beside_ref[0].astype(jnp.float32), beside_ref[1].astype(jnp.float32)
    out_ref[0] = (NEAR[0] * re - NEAR[1] * im + FAR * bre).astype(jnp.bfloat16)
    out_ref[1] = (NEAR[0] * im + NEAR[1] * re + FAR * bim).astype(jnp.bfloat16)


def mix_kernel(scalar_ref, own_ref, beside_ref, across_ref, out_ref):
    centre = scalar_ref[1:2, :]
    for g in range(2):
        rows = slice(16 * g, 16 * g + 16)
        for c in range(COLS):
            at = slice(LANES * c, LANES * c + LANES)
            re, im, bre, bim, are, aim = (
                ref[p, rows, at].astype(jnp.float32) for ref in (own_ref, beside_ref, across_ref) for p in range(2)
            )
            out_ref[0, rows, at] = centre * re - CENTRE[1] * im + (NEAR[0] * bre - NEAR[1] * bim) + FAR * are
            out_ref[1, rows, at] = centre * im + CENTRE[1] * re + (NEAR[0] * bim + NEAR[1] * bre) + FAR * aim


def x_kernel(scalar_ref, mixed_ref, near_ref, fwd_ref, inv_ref, tw_ref, wave_ref, rows_ref, step_ref, out_ref, swept):
    pairs = {}

    def load(g, c):
        at = slice(LANES * c, LANES * c + LANES)
        if g % 2 == 0:
            pairs[c] = near_ref[:, 8 * g : 8 * g + 16, at].astype(jnp.float32)
        rows = slice(8 * g, 8 * g + 8)
        return tuple(mixed_ref[p, rows, at] + pairs[c][p, 8 * (g % 2) : 8 * (g % 2) + 8] for p in range(2))

    def store(g, c, re, im):
        swept[c, 0, g] = re
        swept[c, 1, g] = im

    sweep(load, store, scalar_ref[0:1, :], fwd_ref, inv_ref, tw_ref, tw_ref, wave_ref, rows_ref, step_ref, 1.0)
    for c in range(COLS):
        re = swap_blocks([swept[c, 0, g] for g in range(GROUPS)])
        im = swap_blocks([swept[c, 1, g] for g in range(GROUPS)])
        for q in range(4):
            out_ref[4 * c + q] = jnp.concatenate([re[q], im[q]], axis=0).astype(jnp.bfloat16)


def y_kernel(scalar_ref, in_ref, fwd_ref, inv_ref, tw_f_ref, tw_i_ref, wave_ref, rows_ref, step_ref, out_hbm, field, out_ref, sems):
    for s in range(4):
        block = in_ref[16 * s : 16 * s + 16].astype(jnp.float32)
        for p in range(2):
            flipped = jnp.transpose(block[:, 8 * p : 8 * p + 8, :].reshape(LANES, LANES))
            for x in range(4):
                parts = swap_blocks([flipped[32 * g + 8 * x : 32 * g + 8 * x + 8] for g in range(4)])
                for a in range(4):
                    field[p, 8 * x : 8 * x + 8, LANES * (4 * s + a) : LANES * (4 * s + a + 1)] = parts[a]

    def load(g, c):
        at = slice(LANES * c, LANES * c + LANES)
        return field[0, 8 * g : 8 * g + 8, at], field[1, 8 * g : 8 * g + 8, at]

    def store(g, c, re, im):
        at = slice(LANES * c, LANES * c + LANES)
        out_ref[0, 8 * g : 8 * g + 8, at] = re
        out_ref[1, 8 * g : 8 * g + 8, at] = im

    copies = []

    def send(g):
        rows = slice(8 * g, 8 * g + 8)
        for p in range(2):
            copies.append(pltpu.make_async_copy(out_ref.at[p, rows], out_hbm.at[p, 0, rows], sems.at[g, p]))
            copies[-1].start()

    sweep(load, store, scalar_ref[0:1, :], fwd_ref, inv_ref, tw_f_ref, tw_i_ref, wave_ref, rows_ref, step_ref, -1.0, send)
    for copy in copies:
        copy.wait()


HBM = pl.BlockSpec(memory_space=pltpu.HBM)
VMEM = pl.BlockSpec(memory_space=pltpu.VMEM)
PARAMS = pltpu.CompilerParams(vmem_limit_bytes=48 * 1024 * 1024)


def on_device(wave, potential):
    t = tables()
    f32, bf16 = jnp.float32, jnp.bfloat16
    row_base = lax.axis_index("wa") * ROWS - GRID // 2
    plane = lax.axis_index("gz")
    edge = (plane == 0) | (plane == 7)
    scalars = jnp.stack([row_base.astype(f32) * spacing, jnp.where(edge, CENTRE_EDGE, CENTRE[0])])
    scalars = jnp.broadcast_to(scalars[:, None], (2, LANES))
    own = pl.pallas_call(
        potential_kernel,
        out_shape=jax.ShapeDtypeStruct((2, ROWS, GRID), bf16),
        in_specs=[HBM, HBM],
        out_specs=VMEM,
        scratch_shapes=[
            pltpu.VMEM((2, ROWS, GRID), f32),
            pltpu.VMEM((ROWS, GRID), f32),
            pltpu.SemaphoreType.DMA((4, 3)),
        ],
        compiler_params=PARAMS,
    )(pltpu.with_memory_space_constraint(wave, pltpu.HBM), pltpu.with_memory_space_constraint(potential, pltpu.HBM))
    outward = [(i, i - 1) for i in (2, 4, 6)] + [(i, i + 1) for i in (1, 3, 5)]
    inward = [(i, i + 2) for i in (0, 2, 4)] + [(i, i - 2) for i in (3, 5, 7)]
    beside = lax.ppermute(own, "gz", outward)
    across = lax.ppermute(own, "gz", inward)
    message = pl.pallas_call(
        message_kernel,
        out_shape=jax.ShapeDtypeStruct((2, ROWS, GRID), bf16),
        in_specs=[VMEM, VMEM],
        out_specs=VMEM,
        compiler_params=PARAMS,
    )(own, beside)
    near = lax.ppermute(message, "gz", [(i, i ^ 1) for i in range(8)])
    mixed = pl.pallas_call(
        mix_kernel,
        out_shape=jax.ShapeDtypeStruct((2, ROWS, GRID), f32),
        in_specs=[VMEM] * 4,
        out_specs=VMEM,
        compiler_params=PARAMS,
    )(scalars, own, beside, across)
    chunks = pl.pallas_call(
        x_kernel,
        out_shape=jax.ShapeDtypeStruct((PARTS_WA, 16, LANES), bf16),
        in_specs=[VMEM] * 9,
        out_specs=VMEM,
        scratch_shapes=[
            pltpu.VMEM((COLS, 2, GROUPS, 8, LANES), f32),
        ],
        compiler_params=PARAMS,
    )(scalars, mixed, near, t["fwd_x"], t["inv"], t["tw_x"], t["wavenum"], t["own"], t["step8"])
    chunks = lax.all_to_all(chunks, "wa", 0, 0, tiled=True)
    return pl.pallas_call(
        y_kernel,
        out_shape=jax.ShapeDtypeStruct((2, 1, ROWS, GRID), f32),
        in_specs=[VMEM] * 9,
        out_specs=HBM,
        scratch_shapes=[
            pltpu.VMEM((2, ROWS, GRID), f32),
            pltpu.VMEM((2, ROWS, GRID), f32),
            pltpu.SemaphoreType.DMA((GROUPS, 2)),
        ],
        compiler_params=PARAMS,
    )(scalars, chunks, t["fwd_y"], t["inv"], t["tw_y"], t["tw_x"], t["wavenum"], t["own"], t["step8"])


def solution(mesh):
    in_specs = (P(None, "gz", "wa", None), P("gz", "wa", None))
    out_specs = P(None, "gz", "wa", None)
    return jax.shard_map(
        on_device, mesh=mesh, in_specs=in_specs, out_specs=out_specs, check_vma=False
    )
```

```python
import math

import jax
import jax.numpy as jnp
import numpy as np
from jax import lax
from jax.experimental import pallas as pl
from jax.experimental.pallas import tpu as pltpu
from jax.sharding import PartitionSpec as P

time_step = 0.001
spacing = 1.0 / 32.0
rotation = 0.9
coupling = 400.0
z_coupling = 0.25

GRID = 2048
LANES = 128
COLS = 16
ROWS = 32
GROUPS = 4
PARTS_WA = 64

NEAR = (2.0 * z_coupling * z_coupling, z_coupling)
FAR = -0.5 * z_coupling * z_coupling
CENTRE = (1.0 - 3.0 * z_coupling * z_coupling, -2.0 * z_coupling)
CENTRE_EDGE = 1.0 - 2.5 * z_coupling * z_coupling


def tables():
    lane = np.arange(LANES)
    turned_lane = 32 * ((lane // 16) % 4) + 16 * (lane // 64) + lane % 16
    scale = 1.0 / math.sqrt(GRID)

    def matrices(order):
        angle = 2.0 * np.pi * ((order[:, None] * lane[None, :]) % LANES) / LANES
        cos, sin = np.cos(angle) * scale, np.sin(angle) * scale
        forward = np.block([[cos, -sin], [sin, cos]])
        return forward

    def split(matrix):
        high = matrix.astype(jnp.bfloat16)
        low = (matrix - high.astype(np.float64)).astype(jnp.bfloat16)
        return np.concatenate([np.asarray(high), np.asarray(low)])

    def twiddle(order):
        angle = 2.0 * np.pi * np.arange(COLS)[:, None] * order[None, :] / GRID
        return np.stack([np.cos(angle), np.sin(angle)]).astype(np.float32)

    angle = 2.0 * np.pi * ((lane[:, None] * lane[None, :]) % LANES) / LANES
    cos, sin = np.cos(angle) * scale, np.sin(angle) * scale
    backward = split(np.block([[cos, sin], [-sin, cos]]))
    mode = np.arange(COLS)[:, None] + COLS * lane[None, :]
    signed = np.where(mode < GRID // 2, mode, mode - GRID).astype(np.float64)
    wavenum = signed * (2.0 * np.pi / (GRID * spacing))
    slope = time_step * rotation * spacing * wavenum
    rows8 = slope[:, None, :] * np.arange(8)[None, :, None]
    own = np.stack([np.cos(rows8), np.sin(rows8)]).astype(np.float32)
    step8 = np.stack([np.cos(8.0 * slope), np.sin(8.0 * slope)]).astype(np.float32)
    return {
        "fwd_x": split(matrices(lane)),
        "fwd_y": split(matrices(turned_lane)),
        "inv": backward,
        "small": np.concatenate([twiddle(lane), twiddle(turned_lane), step8, wavenum[None].astype(np.float32)]),
        "own": own,
    }


TWIDDLE, TWIDDLE_TURNED, STEP8, WAVENUM = 0, 2, 4, 6


SINE = (6.283182621002197, -41.34142303466797, 81.59618377685547, -76.5801010131836, 41.205387115478516, -12.271249771118164)
COSINE = (0.9999992251396179, -19.738983154296875, 64.92872619628906, -85.27239227294922, 58.794029235839844, -21.076766967773438)


def sincos(angle):
    turns = angle * (0.5 / math.pi)
    rest = turns - jnp.floor(turns + 0.5)
    square = rest * rest
    sine, cosine = SINE[-1], COSINE[-1]
    for first, second in zip(SINE[-2::-1], COSINE[-2::-1]):
        sine = sine * square + first
        cosine = cosine * square + second
    return sine * rest, cosine


def dft4(v, sign):
    (ar, ai), (br, bi), (cr, ci), (dr, di) = v
    sr, si, tr, ti = ar + cr, ai + ci, ar - cr, ai - ci
    ur, ui, wr, wi = br + dr, bi + di, br - dr, bi - di
    if sign > 0:
        p, q = (tr + wi, ti - wr), (tr - wi, ti + wr)
    else:
        p, q = (tr - wi, ti + wr), (tr + wi, ti - wr)
    return [(sr + ur, si + ui), p, (sr - ur, si - ui), q]


def turn16(v, power, sign):
    power %= 16
    re, im = v
    if power == 0:
        return v
    c, s = math.cos(2.0 * math.pi * power / 16), -sign * math.sin(2.0 * math.pi * power / 16)
    if power == 4:
        return (im, -re) if sign > 0 else (-im, re)
    if power % 2 == 0:
        h = math.sqrt(0.5)
        return (h * (_pm(re, c) + _pm(im, -s)), h * (_pm(re, s) + _pm(im, c)))
    return (re * c - im * s, re * s + im * c)


def _pm(x, sign):
    return x if sign > 0 else -x


def dft16(v, sign):
    low = [dft4([v[4 * a + b] for a in range(4)], sign) for b in range(4)]
    out = [None] * 16
    for k in range(4):
        high = dft4([turn16(low[b][k], b * k, sign) for b in range(4)], sign)
        for k2 in range(4):
            out[k + 4 * k2] = high[k2]
    return out


def exchange(first, second, width):
    upper = (lax.broadcasted_iota(jnp.int32, first.shape, 1) // width) % 2 == 1
    a = jnp.where(upper, pltpu.roll(second, width, 1), first)
    b = jnp.where(upper, second, pltpu.roll(first, LANES - width, 1))
    return a, b


def swap_blocks(v):
    v0, v2 = exchange(v[0], v[2], 64)
    v1, v3 = exchange(v[1], v[3], 64)
    v0, v1 = exchange(v0, v1, 32)
    v2, v3 = exchange(v2, v3, 32)
    return [v0, v1, v2, v3]


def row_phases(first_row, wavenum, step8, sign):
    angle = time_step * (0.5 * wavenum * wavenum + (sign * rotation * first_row) * wavenum)
    sine, cosine = sincos(angle)
    re, im = cosine, -sine
    sr, si = step8[0], -sign * step8[1]
    out = [(re, im)]
    for _ in range(GROUPS - 1):
        re, im = re * sr - im * si, re * si + im * sr
        out.append((re, im))
    return out


def matrix_stage(re, im, table_ref):
    left = jnp.concatenate(
        [
            jnp.concatenate([jnp.concatenate([part[g][m] for g in range(GROUPS)], axis=0) for part in (re, im)], axis=1)
            for m in range(COLS)
        ],
        axis=0,
    ).astype(jnp.bfloat16)
    left = jnp.concatenate([left, left], axis=1)
    return jnp.dot(left, table_ref[...], preferred_element_type=jnp.float32)


def sweep(load, store, first_row, fwd_ref, inv_ref, small_ref, rows_ref, forward, sign, finish=None):
    def parts_of(value, m, g):
        rows = slice(ROWS * m + 8 * g, ROWS * m + 8 * g + 8)
        return value[rows, :LANES], value[rows, LANES:]

    re_in, im_in = [], []
    for g in range(GROUPS):
        out = dft16([load(g, c) for c in range(COLS)], 1)
        for m in range(1, COLS):
            re, im = out[m]
            c, s = small_ref[forward, m : m + 1, :], small_ref[forward + 1, m : m + 1, :]
            out[m] = (re * c + im * s, im * c - re * s)
        re_in.append([v[0] for v in out])
        im_in.append([v[1] for v in out])
    spectrum = matrix_stage(re_in, im_in, fwd_ref)
    phases = row_phases(first_row, small_ref[WAVENUM], small_ref[STEP8 : STEP8 + 2], sign)
    re_in, im_in = [[None] * COLS for _ in range(GROUPS)], [[None] * COLS for _ in range(GROUPS)]
    for m in range(COLS):
        own_re, own_im = rows_ref[0, m], -sign * rows_ref[1, m]
        for g in range(GROUPS):
            row_re, row_im = phases[g][0][m : m + 1, :], phases[g][1][m : m + 1, :]
            f_re, f_im = own_re * row_re - own_im * row_im, own_re * row_im + own_im * row_re
            re, im = parts_of(spectrum, m, g)
            re_in[g][m], im_in[g][m] = re * f_re - im * f_im, re * f_im + im * f_re
    turned = matrix_stage(re_in, im_in, inv_ref)
    for g in range(GROUPS):
        terms = []
        for m in range(COLS):
            re, im = parts_of(turned, m, g)
            if m > 0:
                c, s = small_ref[TWIDDLE, m : m + 1, :], small_ref[TWIDDLE + 1, m : m + 1, :]
                re, im = re * c - im * s, im * c + re * s
            terms.append((re, im))
        for c, (re, im) in enumerate(dft16(terms, -1)):
            store(g, c, re, im)
        if finish is not None:
            finish(g)


def potential_kernel(wave_hbm, potential_hbm, out_ref, wave_ref, potential_ref, sems):
    half = GRID // 2
    blocks = [(slice(16 * g, 16 * g + 16), slice(half * h, half * h + half)) for g in range(2) for h in range(2)]
    copies = []
    for b, (rows, at) in enumerate(blocks):
        copies.append([
            pltpu.make_async_copy(wave_hbm.at[:, 0, rows, at], wave_ref.at[:, rows, at], sems.at[b, 0]),
            pltpu.make_async_copy(potential_hbm.at[0, rows, at], potential_ref.at[rows, at], sems.at[b, 1]),
        ])
        for copy in copies[-1]:
            copy.start()
    for (rows, at), waits in zip(blocks, copies):
        for copy in waits:
            copy.wait()
        for first in range(at.start, at.stop, LANES):
            cols = slice(first, first + LANES)
            re, im, pot = wave_ref[0, rows, cols], wave_ref[1, rows, cols], potential_ref[rows, cols]
            sine, cosine = sincos(time_step * (pot + coupling * (re * re + im * im)))
            out_ref[0, rows, cols] = (re * cosine + im * sine).astype(jnp.bfloat16)
            out_ref[1, rows, cols] = (im * cosine - re * sine).astype(jnp.bfloat16)


def message_kernel(own_ref, beside_ref, out_ref):
    re, im = own_ref[0].astype(jnp.float32), own_ref[1].astype(jnp.float32)
    bre, bim = beside_ref[0].astype(jnp.float32), beside_ref[1].astype(jnp.float32)
    out_ref[0] = (NEAR[0] * re - NEAR[1] * im + FAR * bre).astype(jnp.bfloat16)
    out_ref[1] = (NEAR[0] * im + NEAR[1] * re + FAR * bim).astype(jnp.bfloat16)


def mix_kernel(scalar_ref, own_ref, beside_ref, across_ref, out_ref):
    centre = scalar_ref[1:2, :]
    for g in range(2):
        rows = slice(16 * g, 16 * g + 16)
        for c in range(COLS):
            at = slice(LANES * c, LANES * c + LANES)
            re, im, bre, bim, are, aim = (
                ref[p, rows, at].astype(jnp.float32) for ref in (own_ref, beside_ref, across_ref) for p in range(2)
            )
            out_ref[0, rows, at] = centre * re - CENTRE[1] * im + (NEAR[0] * bre - NEAR[1] * bim) + FAR * are
            out_ref[1, rows, at] = centre * im + CENTRE[1] * re + (NEAR[0] * bim + NEAR[1] * bre) + FAR * aim


def x_kernel(scalar_ref, mixed_ref, near_ref, fwd_ref, inv_ref, small_ref, rows_ref, out_ref, swept):
    pairs = {}

    def load(g, c):
        at = slice(LANES * c, LANES * c + LANES)
        if g % 2 == 0:
            pairs[c] = near_ref[:, 8 * g : 8 * g + 16, at].astype(jnp.float32)
        rows = slice(8 * g, 8 * g + 8)
        return tuple(mixed_ref[p, rows, at] + pairs[c][p, 8 * (g % 2) : 8 * (g % 2) + 8] for p in range(2))

    def store(g, c, re, im):
        swept[c, 0, 8 * g : 8 * g + 8] = re
        swept[c, 1, 8 * g : 8 * g + 8] = im

    sweep(load, store, scalar_ref[0:1, :], fwd_ref, inv_ref, small_ref, rows_ref, TWIDDLE, 1.0)
    for c in range(COLS):
        tiles = swap_blocks([swept[c, p, 16 * h : 16 * h + 16] for p in range(2) for h in range(2)])
        for q in range(4):
            out_ref[4 * c + q] = tiles[q].astype(jnp.bfloat16)


def y_kernel(scalar_ref, in_ref, fwd_ref, inv_ref, small_ref, rows_ref, out_hbm, field, out_ref, sems):
    for s in range(8):
        flipped = jnp.transpose(in_ref[8 * s : 8 * s + 8].reshape(LANES, LANES)).astype(jnp.float32)
        for p in range(2):
            for x in range(4):
                rows = slice(8 * x, 8 * x + 8)
                low, high = (flipped[64 * p + 32 * h + 8 * x : 64 * p + 32 * h + 8 * x + 8] for h in range(2))
                low, high = exchange(low, high, 64)
                field[p, rows, LANES * (2 * s) : LANES * (2 * s + 1)] = low
                field[p, rows, LANES * (2 * s + 1) : LANES * (2 * s + 2)] = high

    def load(g, c):
        at = slice(LANES * c, LANES * c + LANES)
        return field[0, 8 * g : 8 * g + 8, at], field[1, 8 * g : 8 * g + 8, at]

    def store(g, c, re, im):
        at = slice(LANES * c, LANES * c + LANES)
        out_ref[0, 8 * g : 8 * g + 8, at] = re
        out_ref[1, 8 * g : 8 * g + 8, at] = im

    copies = []

    def send(g):
        rows = slice(8 * g, 8 * g + 8)
        for p in range(2):
            copies.append(pltpu.make_async_copy(out_ref.at[p, rows], out_hbm.at[p, 0, rows], sems.at[g, p]))
            copies[-1].start()

    sweep(load, store, scalar_ref[0:1, :], fwd_ref, inv_ref, small_ref, rows_ref, TWIDDLE_TURNED, -1.0, send)
    for copy in copies:
        copy.wait()


HBM = pl.BlockSpec(memory_space=pltpu.HBM)
VMEM = pl.BlockSpec(memory_space=pltpu.VMEM)
PARAMS = pltpu.CompilerParams(vmem_limit_bytes=48 * 1024 * 1024)


def on_device(wave, potential):
    t = tables()
    f32, bf16 = jnp.float32, jnp.bfloat16
    row_base = lax.axis_index("wa") * ROWS - GRID // 2
    plane = lax.axis_index("gz")
    edge = (plane == 0) | (plane == 7)
    scalars = jnp.stack([row_base.astype(f32) * spacing, jnp.where(edge, CENTRE_EDGE, CENTRE[0])])
    scalars = jnp.broadcast_to(scalars[:, None], (2, LANES))
    own = pl.pallas_call(
        potential_kernel,
        out_shape=jax.ShapeDtypeStruct((2, ROWS, GRID), bf16),
        in_specs=[HBM, HBM],
        out_specs=VMEM,
        scratch_shapes=[
            pltpu.VMEM((2, ROWS, GRID), f32),
            pltpu.VMEM((ROWS, GRID), f32),
            pltpu.SemaphoreType.DMA((4, 2)),
        ],
        compiler_params=PARAMS,
    )(pltpu.with_memory_space_constraint(wave, pltpu.HBM), pltpu.with_memory_space_constraint(potential, pltpu.HBM))
    outward = [(i, i - 1) for i in (2, 4, 6)] + [(i, i + 1) for i in (1, 3, 5)]
    inward = [(i, i + 2) for i in (0, 2, 4)] + [(i, i - 2) for i in (3, 5, 7)]
    beside = lax.ppermute(own, "gz", outward)
    across = lax.ppermute(own, "gz", inward)
    message = pl.pallas_call(
        message_kernel,
        out_shape=jax.ShapeDtypeStruct((2, ROWS, GRID), bf16),
        in_specs=[VMEM, VMEM],
        out_specs=VMEM,
        compiler_params=PARAMS,
    )(own, beside)
    near = lax.ppermute(message, "gz", [(i, i ^ 1) for i in range(8)])
    mixed = pl.pallas_call(
        mix_kernel,
        out_shape=jax.ShapeDtypeStruct((2, ROWS, GRID), f32),
        in_specs=[VMEM] * 4,
        out_specs=VMEM,
        compiler_params=PARAMS,
    )(scalars, own, beside, across)
    chunks = pl.pallas_call(
        x_kernel,
        out_shape=jax.ShapeDtypeStruct((PARTS_WA, 16, LANES), bf16),
        in_specs=[VMEM] * 7,
        out_specs=VMEM,
        scratch_shapes=[
            pltpu.VMEM((COLS, 2, ROWS, LANES), f32),
        ],
        compiler_params=PARAMS,
    )(scalars, mixed, near, t["fwd_x"], t["inv"], t["small"], t["own"])
    chunks = lax.all_to_all(chunks, "wa", 0, 0, tiled=True)
    return pl.pallas_call(
        y_kernel,
        out_shape=jax.ShapeDtypeStruct((2, 1, ROWS, GRID), f32),
        in_specs=[VMEM] * 6,
        out_specs=HBM,
        scratch_shapes=[
            pltpu.VMEM((2, ROWS, GRID), f32),
            pltpu.VMEM((2, ROWS, GRID), f32),
            pltpu.SemaphoreType.DMA((GROUPS, 2)),
        ],
        compiler_params=PARAMS,
    )(scalars, chunks, t["fwd_y"], t["inv"], t["small"], t["own"])


def solution(mesh):
    in_specs = (P(None, "gz", "wa", None), P("gz", "wa", None))
    out_specs = P(None, "gz", "wa", None)
    return jax.shard_map(
        on_device, mesh=mesh, in_specs=in_specs, out_specs=out_specs, check_vma=False
    )
```

```python
import math

import jax
import jax.numpy as jnp
import numpy as np
from jax import lax
from jax.experimental import pallas as pl
from jax.experimental.pallas import tpu as pltpu
from jax.sharding import PartitionSpec as P

time_step = 0.001
spacing = 1.0 / 32.0
rotation = 0.9
coupling = 400.0
z_coupling = 0.25

GRID = 2048
LANES = 128
COLS = 16
ROWS = 32
GROUPS = 4
PARTS_WA = 64

NEAR = (2.0 * z_coupling * z_coupling, z_coupling)
FAR = -0.5 * z_coupling * z_coupling
CENTRE = (1.0 - 3.0 * z_coupling * z_coupling, -2.0 * z_coupling)
CENTRE_EDGE = 1.0 - 2.5 * z_coupling * z_coupling


def tables():
    lane = np.arange(LANES)
    turned_lane = 32 * ((lane // 16) % 4) + 16 * (lane // 64) + lane % 16
    scale = 1.0 / math.sqrt(GRID)

    def matrices(order):
        angle = 2.0 * np.pi * ((order[:, None] * lane[None, :]) % LANES) / LANES
        cos, sin = np.cos(angle) * scale, np.sin(angle) * scale
        forward = np.block([[cos, -sin], [sin, cos]])
        return forward

    def split(matrix):
        high = matrix.astype(jnp.bfloat16)
        low = (matrix - high.astype(np.float64)).astype(jnp.bfloat16)
        return np.concatenate([np.asarray(high), np.asarray(low)])

    def twiddle(order):
        angle = 2.0 * np.pi * np.arange(COLS)[:, None] * order[None, :] / GRID
        return np.stack([np.cos(angle), np.sin(angle)]).astype(np.float32)

    angle = 2.0 * np.pi * ((lane[:, None] * lane[None, :]) % LANES) / LANES
    cos, sin = np.cos(angle) * scale, np.sin(angle) * scale
    backward = split(np.block([[cos, sin], [-sin, cos]]))
    mode = np.arange(COLS)[:, None] + COLS * lane[None, :]
    signed = np.where(mode < GRID // 2, mode, mode - GRID).astype(np.float64)
    wavenum = signed * (2.0 * np.pi / (GRID * spacing))
    slope = time_step * rotation * spacing * wavenum
    rows8 = slope[:, None, :] * np.arange(8)[None, :, None]
    own = np.stack([np.cos(rows8), np.sin(rows8)]).astype(np.float32)
    step8 = np.stack([np.cos(8.0 * slope), np.sin(8.0 * slope)]).astype(np.float32)
    return {
        "fwd_x": split(matrices(lane)),
        "fwd_y": split(matrices(turned_lane)),
        "inv": backward,
        "small": np.concatenate([twiddle(lane), twiddle(turned_lane), step8, wavenum[None].astype(np.float32)]),
        "own": own,
    }


TWIDDLE, TWIDDLE_TURNED, STEP8, WAVENUM = 0, 2, 4, 6


SINE = (6.283182621002197, -41.34142303466797, 81.59618377685547, -76.5801010131836, 41.205387115478516, -12.271249771118164)
COSINE = (0.9999992251396179, -19.738983154296875, 64.92872619628906, -85.27239227294922, 58.794029235839844, -21.076766967773438)


def sincos(angle):
    turns = angle * (0.5 / math.pi)
    rest = turns - jnp.floor(turns + 0.5)
    square = rest * rest
    sine, cosine = SINE[-1], COSINE[-1]
    for first, second in zip(SINE[-2::-1], COSINE[-2::-1]):
        sine = sine * square + first
        cosine = cosine * square + second
    return sine * rest, cosine


def dft4(v, sign):
    (ar, ai), (br, bi), (cr, ci), (dr, di) = v
    sr, si, tr, ti = ar + cr, ai + ci, ar - cr, ai - ci
    ur, ui, wr, wi = br + dr, bi + di, br - dr, bi - di
    if sign > 0:
        p, q = (tr + wi, ti - wr), (tr - wi, ti + wr)
    else:
        p, q = (tr - wi, ti + wr), (tr + wi, ti - wr)
    return [(sr + ur, si + ui), p, (sr - ur, si - ui), q]


def turn16(v, power, sign):
    power %= 16
    re, im = v
    if power == 0:
        return v
    c, s = math.cos(2.0 * math.pi * power / 16), -sign * math.sin(2.0 * math.pi * power / 16)
    if power == 4:
        return (im, -re) if sign > 0 else (-im, re)
    if power % 2 == 0:
        h = math.sqrt(0.5)
        return (h * (_pm(re, c) + _pm(im, -s)), h * (_pm(re, s) + _pm(im, c)))
    return (re * c - im * s, re * s + im * c)


def _pm(x, sign):
    return x if sign > 0 else -x


def dft16(v, sign):
    low = [dft4([v[4 * a + b] for a in range(4)], sign) for b in range(4)]
    out = [None] * 16
    for k in range(4):
        high = dft4([turn16(low[b][k], b * k, sign) for b in range(4)], sign)
        for k2 in range(4):
            out[k + 4 * k2] = high[k2]
    return out


def exchange(first, second, width):
    upper = (lax.broadcasted_iota(jnp.int32, first.shape, 1) // width) % 2 == 1
    a = jnp.where(upper, pltpu.roll(second, width, 1), first)
    b = jnp.where(upper, second, pltpu.roll(first, LANES - width, 1))
    return a, b


def swap_blocks(v):
    v0, v2 = exchange(v[0], v[2], 64)
    v1, v3 = exchange(v[1], v[3], 64)
    v0, v1 = exchange(v0, v1, 32)
    v2, v3 = exchange(v2, v3, 32)
    return [v0, v1, v2, v3]


def row_phases(first_row, wavenum, step8, sign):
    angle = time_step * (0.5 * wavenum * wavenum + (sign * rotation * first_row) * wavenum)
    sine, cosine = sincos(angle)
    re, im = cosine, -sine
    sr, si = step8[0], -sign * step8[1]
    out = [(re, im)]
    for _ in range(GROUPS - 1):
        re, im = re * sr - im * si, re * si + im * sr
        out.append((re, im))
    return out


def matrix_stage(re, im, table_ref):
    left = jnp.concatenate(
        [
            jnp.concatenate([jnp.concatenate([group[m] for group in part], axis=0) for part in (re, im)], axis=1)
            for m in range(COLS)
        ],
        axis=0,
    ).astype(jnp.bfloat16)
    left = jnp.concatenate([left, left], axis=1)
    return jnp.dot(left, table_ref[...], preferred_element_type=jnp.float32)


def sweep(load, store, first_row, fwd_ref, inv_ref, small_ref, rows_ref, forward, sign, finish=None):
    phases = row_phases(first_row, small_ref[WAVENUM], small_ref[STEP8 : STEP8 + 2], sign)

    def parts_of(value, m):
        rows = slice(8 * m, 8 * m + 8)
        return value[rows, :LANES], value[rows, LANES:]

    def first(groups):
        re_in, im_in = [], []
        for g in groups:
            out = dft16([load(g, c) for c in range(COLS)], 1)
            for m in range(1, COLS):
                re, im = out[m]
                c, s = small_ref[forward, m : m + 1, :], small_ref[forward + 1, m : m + 1, :]
                out[m] = (re * c + im * s, im * c - re * s)
            re_in.append([v[0] for v in out])
            im_in.append([v[1] for v in out])
        return matrix_stage(re_in, im_in, fwd_ref)

    def second(groups, spectrum):
        re_in, im_in = [[None] * COLS for _ in groups], [[None] * COLS for _ in groups]
        for m in range(COLS):
            own_re, own_im = rows_ref[0, m], -sign * rows_ref[1, m]
            for i, g in enumerate(groups):
                row_re, row_im = phases[g][0][m : m + 1, :], phases[g][1][m : m + 1, :]
                f_re, f_im = own_re * row_re - own_im * row_im, own_re * row_im + own_im * row_re
                re, im = parts_of(spectrum, m)
                re_in[i][m], im_in[i][m] = re * f_re - im * f_im, re * f_im + im * f_re
        return matrix_stage(re_in, im_in, inv_ref)

    def third(groups, turned):
        for i, g in enumerate(groups):
            terms = []
            for m in range(COLS):
                re, im = parts_of(turned, m)
                if m > 0:
                    c, s = small_ref[TWIDDLE, m : m + 1, :], small_ref[TWIDDLE + 1, m : m + 1, :]
                    re, im = re * c - im * s, im * c + re * s
                terms.append((re, im))
            for c, (re, im) in enumerate(dft16(terms, -1)):
                store(g, c, re, im)
            if finish is not None:
                finish(g)

    for g in range(GROUPS):
        groups = (g,)
        third(groups, second(groups, first(groups)))

def potential_kernel(wave_hbm, potential_hbm, out_ref, wave_ref, potential_ref, sems):
    half = GRID // 2
    blocks = [(slice(16 * g, 16 * g + 16), slice(half * h, half * h + half)) for g in range(2) for h in range(2)]
    copies = []
    for b, (rows, at) in enumerate(blocks):
        copies.append([
            pltpu.make_async_copy(wave_hbm.at[:, 0, rows, at], wave_ref.at[:, rows, at], sems.at[b, 0]),
            pltpu.make_async_copy(potential_hbm.at[0, rows, at], potential_ref.at[rows, at], sems.at[b, 1]),
        ])
        for copy in copies[-1]:
            copy.start()
    for (rows, at), waits in zip(blocks, copies):
        for copy in waits:
            copy.wait()
        for first in range(at.start, at.stop, LANES):
            cols = slice(first, first + LANES)
            re, im, pot = wave_ref[0, rows, cols], wave_ref[1, rows, cols], potential_ref[rows, cols]
            sine, cosine = sincos(time_step * (pot + coupling * (re * re + im * im)))
            out_ref[0, rows, cols] = (re * cosine + im * sine).astype(jnp.bfloat16)
            out_ref[1, rows, cols] = (im * cosine - re * sine).astype(jnp.bfloat16)


def message_kernel(own_ref, beside_ref, out_ref):
    re, im = own_ref[0].astype(jnp.float32), own_ref[1].astype(jnp.float32)
    bre, bim = beside_ref[0].astype(jnp.float32), beside_ref[1].astype(jnp.float32)
    out_ref[0] = (NEAR[0] * re - NEAR[1] * im + FAR * bre).astype(jnp.bfloat16)
    out_ref[1] = (NEAR[0] * im + NEAR[1] * re + FAR * bim).astype(jnp.bfloat16)


def mix_kernel(scalar_ref, own_ref, beside_ref, across_ref, out_ref):
    centre = scalar_ref[1:2, :]
    for g in range(2):
        rows = slice(16 * g, 16 * g + 16)
        for c in range(COLS):
            at = slice(LANES * c, LANES * c + LANES)
            re, im, bre, bim, are, aim = (
                ref[p, rows, at].astype(jnp.float32) for ref in (own_ref, beside_ref, across_ref) for p in range(2)
            )
            out_ref[0, rows, at] = centre * re - CENTRE[1] * im + (NEAR[0] * bre - NEAR[1] * bim) + FAR * are
            out_ref[1, rows, at] = centre * im + CENTRE[1] * re + (NEAR[0] * bim + NEAR[1] * bre) + FAR * aim


def x_kernel(scalar_ref, mixed_ref, near_ref, fwd_ref, inv_ref, small_ref, rows_ref, out_ref, swept):
    pairs = {}

    def load(g, c):
        at = slice(LANES * c, LANES * c + LANES)
        if g % 2 == 0:
            pairs[c] = near_ref[:, 8 * g : 8 * g + 16, at].astype(jnp.float32)
        rows = slice(8 * g, 8 * g + 8)
        return tuple(mixed_ref[p, rows, at] + pairs[c][p, 8 * (g % 2) : 8 * (g % 2) + 8] for p in range(2))

    def store(g, c, re, im):
        swept[c, 0, 8 * g : 8 * g + 8] = re
        swept[c, 1, 8 * g : 8 * g + 8] = im

    sweep(load, store, scalar_ref[0:1, :], fwd_ref, inv_ref, small_ref, rows_ref, TWIDDLE, 1.0)
    for c in range(COLS):
        tiles = swap_blocks([swept[c, p, 16 * h : 16 * h + 16] for p in range(2) for h in range(2)])
        for q in range(4):
            out_ref[4 * c + q] = tiles[q].astype(jnp.bfloat16)


def y_kernel(scalar_ref, in_ref, fwd_ref, inv_ref, small_ref, rows_ref, out_hbm, field, out_ref, sems):
    for s in range(8):
        flipped = jnp.transpose(in_ref[8 * s : 8 * s + 8].reshape(LANES, LANES)).astype(jnp.float32)
        for p in range(2):
            for x in range(4):
                rows = slice(8 * x, 8 * x + 8)
                low, high = (flipped[64 * p + 32 * h + 8 * x : 64 * p + 32 * h + 8 * x + 8] for h in range(2))
                low, high = exchange(low, high, 64)
                field[p, rows, LANES * (2 * s) : LANES * (2 * s + 1)] = low
                field[p, rows, LANES * (2 * s + 1) : LANES * (2 * s + 2)] = high

    def load(g, c):
        at = slice(LANES * c, LANES * c + LANES)
        return field[0, 8 * g : 8 * g + 8, at], field[1, 8 * g : 8 * g + 8, at]

    def store(g, c, re, im):
        at = slice(LANES * c, LANES * c + LANES)
        out_ref[0, 8 * g : 8 * g + 8, at] = re
        out_ref[1, 8 * g : 8 * g + 8, at] = im

    copies = []

    def send(g):
        rows = slice(8 * g, 8 * g + 8)
        for p in range(2):
            copies.append(pltpu.make_async_copy(out_ref.at[p, rows], out_hbm.at[p, 0, rows], sems.at[g, p]))
            copies[-1].start()

    sweep(load, store, scalar_ref[0:1, :], fwd_ref, inv_ref, small_ref, rows_ref, TWIDDLE_TURNED, -1.0, send)
    for copy in copies:
        copy.wait()


HBM = pl.BlockSpec(memory_space=pltpu.HBM)
VMEM = pl.BlockSpec(memory_space=pltpu.VMEM)
PARAMS = pltpu.CompilerParams(vmem_limit_bytes=48 * 1024 * 1024)


def on_device(wave, potential):
    t = tables()
    f32, bf16 = jnp.float32, jnp.bfloat16
    row_base = lax.axis_index("wa") * ROWS - GRID // 2
    plane = lax.axis_index("gz")
    edge = (plane == 0) | (plane == 7)
    scalars = jnp.stack([row_base.astype(f32) * spacing, jnp.where(edge, CENTRE_EDGE, CENTRE[0])])
    scalars = jnp.broadcast_to(scalars[:, None], (2, LANES))
    own = pl.pallas_call(
        potential_kernel,
        out_shape=jax.ShapeDtypeStruct((2, ROWS, GRID), bf16),
        in_specs=[HBM, HBM],
        out_specs=VMEM,
        scratch_shapes=[
            pltpu.VMEM((2, ROWS, GRID), f32),
            pltpu.VMEM((ROWS, GRID), f32),
            pltpu.SemaphoreType.DMA((4, 2)),
        ],
        compiler_params=PARAMS,
    )(pltpu.with_memory_space_constraint(wave, pltpu.HBM), pltpu.with_memory_space_constraint(potential, pltpu.HBM))
    outward = [(i, i - 1) for i in (2, 4, 6)] + [(i, i + 1) for i in (1, 3, 5)]
    inward = [(i, i + 2) for i in (0, 2, 4)] + [(i, i - 2) for i in (3, 5, 7)]
    beside = lax.ppermute(own, "gz", outward)
    across = lax.ppermute(own, "gz", inward)
    message = pl.pallas_call(
        message_kernel,
        out_shape=jax.ShapeDtypeStruct((2, ROWS, GRID), bf16),
        in_specs=[VMEM, VMEM],
        out_specs=VMEM,
        compiler_params=PARAMS,
    )(own, beside)
    near = lax.ppermute(message, "gz", [(i, i ^ 1) for i in range(8)])
    mixed = pl.pallas_call(
        mix_kernel,
        out_shape=jax.ShapeDtypeStruct((2, ROWS, GRID), f32),
        in_specs=[VMEM] * 4,
        out_specs=VMEM,
        compiler_params=PARAMS,
    )(scalars, own, beside, across)
    chunks = pl.pallas_call(
        x_kernel,
        out_shape=jax.ShapeDtypeStruct((PARTS_WA, 16, LANES), bf16),
        in_specs=[VMEM] * 7,
        out_specs=VMEM,
        scratch_shapes=[
            pltpu.VMEM((COLS, 2, ROWS, LANES), f32),
        ],
        compiler_params=PARAMS,
    )(scalars, mixed, near, t["fwd_x"], t["inv"], t["small"], t["own"])
    chunks = lax.all_to_all(chunks, "wa", 0, 0, tiled=True)
    return pl.pallas_call(
        y_kernel,
        out_shape=jax.ShapeDtypeStruct((2, 1, ROWS, GRID), f32),
        in_specs=[VMEM] * 6,
        out_specs=HBM,
        scratch_shapes=[
            pltpu.VMEM((2, ROWS, GRID), f32),
            pltpu.VMEM((2, ROWS, GRID), f32),
            pltpu.SemaphoreType.DMA((GROUPS, 2)),
        ],
        compiler_params=PARAMS,
    )(scalars, chunks, t["fwd_y"], t["inv"], t["small"], t["own"])


def solution(mesh):
    in_specs = (P(None, "gz", "wa", None), P("gz", "wa", None))
    out_specs = P(None, "gz", "wa", None)
    return jax.shard_map(
        on_device, mesh=mesh, in_specs=in_specs, out_specs=out_specs, check_vma=False
    )
```

```python
import math

import jax
import jax.numpy as jnp
import numpy as np
from jax import lax
from jax.experimental import pallas as pl
from jax.experimental.pallas import tpu as pltpu
from jax.sharding import PartitionSpec as P

time_step = 0.001
spacing = 1.0 / 32.0
rotation = 0.9
coupling = 400.0
z_coupling = 0.25

GRID = 2048
LANES = 128
COLS = 16
ROWS = 32
GROUPS = 4
PARTS_WA = 64

NEAR = (2.0 * z_coupling * z_coupling, z_coupling)
FAR = -0.5 * z_coupling * z_coupling
CENTRE = (1.0 - 3.0 * z_coupling * z_coupling, -2.0 * z_coupling)
CENTRE_EDGE = 1.0 - 2.5 * z_coupling * z_coupling


def tables():
    lane = np.arange(LANES)
    turned_lane = 32 * ((lane // 16) % 4) + 16 * (lane // 64) + lane % 16
    scale = 1.0 / math.sqrt(GRID)

    def matrices(order):
        angle = 2.0 * np.pi * ((order[:, None] * lane[None, :]) % LANES) / LANES
        cos, sin = np.cos(angle) * scale, np.sin(angle) * scale
        forward = np.block([[cos, -sin], [sin, cos]])
        return forward

    def split(matrix):
        high = matrix.astype(jnp.bfloat16)
        low = (matrix - high.astype(np.float64)).astype(jnp.bfloat16)
        return np.concatenate([np.asarray(high), np.asarray(low)])

    def twiddle(order):
        angle = 2.0 * np.pi * np.arange(COLS)[:, None] * order[None, :] / GRID
        return np.stack([np.cos(angle), np.sin(angle)]).astype(np.float32)

    angle = 2.0 * np.pi * ((lane[:, None] * lane[None, :]) % LANES) / LANES
    cos, sin = np.cos(angle) * scale, np.sin(angle) * scale
    backward = split(np.block([[cos, sin], [-sin, cos]]))
    mode = np.arange(COLS)[:, None] + COLS * lane[None, :]
    signed = np.where(mode < GRID // 2, mode, mode - GRID).astype(np.float64)
    wavenum = signed * (2.0 * np.pi / (GRID * spacing))
    slope = time_step * rotation * spacing * wavenum
    rows8 = slope[:, None, :] * np.arange(8)[None, :, None]
    own = np.stack([np.cos(rows8), np.sin(rows8)]).astype(np.float32)
    step8 = np.stack([np.cos(8.0 * slope), np.sin(8.0 * slope)]).astype(np.float32)
    return {
        "fwd_x": split(matrices(lane)),
        "fwd_y": split(matrices(turned_lane)),
        "inv": backward,
        "small": np.concatenate([twiddle(lane), twiddle(turned_lane), step8, wavenum[None].astype(np.float32)]),
        "own": own,
    }


TWIDDLE, TWIDDLE_TURNED, STEP8, WAVENUM = 0, 2, 4, 6


SINE = (6.283182621002197, -41.34142303466797, 81.59618377685547, -76.5801010131836, 41.205387115478516, -12.271249771118164)
COSINE = (0.9999992251396179, -19.738983154296875, 64.92872619628906, -85.27239227294922, 58.794029235839844, -21.076766967773438)


def sincos(angle):
    turns = angle * (0.5 / math.pi)
    rest = turns - jnp.floor(turns + 0.5)
    square = rest * rest
    sine, cosine = SINE[-1], COSINE[-1]
    for first, second in zip(SINE[-2::-1], COSINE[-2::-1]):
        sine = sine * square + first
        cosine = cosine * square + second
    return sine * rest, cosine


def dft4(v, sign):
    (ar, ai), (br, bi), (cr, ci), (dr, di) = v
    sr, si, tr, ti = ar + cr, ai + ci, ar - cr, ai - ci
    ur, ui, wr, wi = br + dr, bi + di, br - dr, bi - di
    if sign > 0:
        p, q = (tr + wi, ti - wr), (tr - wi, ti + wr)
    else:
        p, q = (tr - wi, ti + wr), (tr + wi, ti - wr)
    return [(sr + ur, si + ui), p, (sr - ur, si - ui), q]


def turn16(v, power, sign):
    power %= 16
    re, im = v
    if power == 0:
        return v
    c, s = math.cos(2.0 * math.pi * power / 16), -sign * math.sin(2.0 * math.pi * power / 16)
    if power == 4:
        return (im, -re) if sign > 0 else (-im, re)
    if power % 2 == 0:
        h = math.sqrt(0.5)
        return (h * (_pm(re, c) + _pm(im, -s)), h * (_pm(re, s) + _pm(im, c)))
    return (re * c - im * s, re * s + im * c)


def _pm(x, sign):
    return x if sign > 0 else -x


def dft16(v, sign):
    low = [dft4([v[4 * a + b] for a in range(4)], sign) for b in range(4)]
    out = [None] * 16
    for k in range(4):
        high = dft4([turn16(low[b][k], b * k, sign) for b in range(4)], sign)
        for k2 in range(4):
            out[k + 4 * k2] = high[k2]
    return out


def exchange(first, second, width):
    upper = (lax.broadcasted_iota(jnp.int32, first.shape, 1) // width) % 2 == 1
    a = jnp.where(upper, pltpu.roll(second, width, 1), first)
    b = jnp.where(upper, second, pltpu.roll(first, LANES - width, 1))
    return a, b


def swap_blocks(v):
    v0, v2 = exchange(v[0], v[2], 64)
    v1, v3 = exchange(v[1], v[3], 64)
    v0, v1 = exchange(v0, v1, 32)
    v2, v3 = exchange(v2, v3, 32)
    return [v0, v1, v2, v3]


def row_phases(first_row, wavenum, step8, sign):
    angle = time_step * (0.5 * wavenum * wavenum + (sign * rotation * first_row) * wavenum)
    sine, cosine = sincos(angle)
    re, im = cosine, -sine
    sr, si = step8[0], -sign * step8[1]
    out = [(re, im)]
    for _ in range(GROUPS - 1):
        re, im = re * sr - im * si, re * si + im * sr
        out.append((re, im))
    return out


def matrix_stage(re, im, table_ref):
    left = jnp.concatenate(
        [
            jnp.concatenate([jnp.concatenate([group[m] for group in part], axis=0) for part in (re, im)], axis=1)
            for m in range(COLS)
        ],
        axis=0,
    ).astype(jnp.bfloat16)
    left = jnp.concatenate([left, left], axis=1)
    return jnp.dot(left, table_ref[...], preferred_element_type=jnp.float32)


def sweep(load, store, first_row, fwd_ref, inv_ref, small_ref, rows_ref, forward, sign, finish=None):
    phases = row_phases(first_row, small_ref[WAVENUM], small_ref[STEP8 : STEP8 + 2], sign)

    def parts_of(value, m):
        rows = slice(8 * m, 8 * m + 8)
        return value[rows, :LANES], value[rows, LANES:]

    def first(groups):
        re_in, im_in = [], []
        for g in groups:
            out = dft16([load(g, c) for c in range(COLS)], 1)
            for m in range(1, COLS):
                re, im = out[m]
                c, s = small_ref[forward, m : m + 1, :], small_ref[forward + 1, m : m + 1, :]
                out[m] = (re * c + im * s, im * c - re * s)
            re_in.append([v[0] for v in out])
            im_in.append([v[1] for v in out])
        return matrix_stage(re_in, im_in, fwd_ref)

    def second(groups, spectrum):
        re_in, im_in = [[None] * COLS for _ in groups], [[None] * COLS for _ in groups]
        for m in range(COLS):
            own_re, own_im = rows_ref[0, m], -sign * rows_ref[1, m]
            for i, g in enumerate(groups):
                row_re, row_im = phases[g][0][m : m + 1, :], phases[g][1][m : m + 1, :]
                f_re, f_im = own_re * row_re - own_im * row_im, own_re * row_im + own_im * row_re
                re, im = parts_of(spectrum, m)
                re_in[i][m], im_in[i][m] = re * f_re - im * f_im, re * f_im + im * f_re
        return matrix_stage(re_in, im_in, inv_ref)

    def third(groups, turned):
        for i, g in enumerate(groups):
            terms = []
            for m in range(COLS):
                re, im = parts_of(turned, m)
                if m > 0:
                    c, s = small_ref[TWIDDLE, m : m + 1, :], small_ref[TWIDDLE + 1, m : m + 1, :]
                    re, im = re * c - im * s, im * c + re * s
                terms.append((re, im))
            for c, (re, im) in enumerate(dft16(terms, -1)):
                store(g, c, re, im)
            if finish is not None:
                finish(g)

    for g in range(GROUPS):
        groups = (g,)
        third(groups, second(groups, first(groups)))

def potential_kernel(wave_hbm, potential_hbm, out_ref, wave_ref, potential_ref, sems):
    half = GRID // 2
    blocks = [(slice(16 * g, 16 * g + 16), slice(half * h, half * h + half)) for g in range(2) for h in range(2)]
    copies = []
    for b, (rows, at) in enumerate(blocks):
        copies.append([
            pltpu.make_async_copy(wave_hbm.at[:, 0, rows, at], wave_ref.at[:, rows, at], sems.at[b, 0]),
            pltpu.make_async_copy(potential_hbm.at[0, rows, at], potential_ref.at[rows, at], sems.at[b, 1]),
        ])
        for copy in copies[-1]:
            copy.start()
    for (rows, at), waits in zip(blocks, copies):
        for copy in waits:
            copy.wait()
        for first in range(at.start, at.stop, LANES):
            cols = slice(first, first + LANES)
            re, im, pot = wave_ref[0, rows, cols], wave_ref[1, rows, cols], potential_ref[rows, cols]
            sine, cosine = sincos(time_step * (pot + coupling * (re * re + im * im)))
            out_ref[0, rows, cols] = (re * cosine + im * sine).astype(jnp.bfloat16)
            out_ref[1, rows, cols] = (im * cosine - re * sine).astype(jnp.bfloat16)


def message_kernel(own_ref, beside_ref, out_ref):
    re, im = own_ref[0].astype(jnp.float32), own_ref[1].astype(jnp.float32)
    bre, bim = beside_ref[0].astype(jnp.float32), beside_ref[1].astype(jnp.float32)
    out_ref[0] = (NEAR[0] * re - NEAR[1] * im + FAR * bre).astype(jnp.bfloat16)
    out_ref[1] = (NEAR[0] * im + NEAR[1] * re + FAR * bim).astype(jnp.bfloat16)


def mix_kernel(scalar_ref, own_ref, beside_ref, across_ref, *tables_and_out):
    out_ref = tables_and_out[-1]
    centre = scalar_ref[1:2, :]
    for g in range(2):
        rows = slice(16 * g, 16 * g + 16)
        for c in range(COLS):
            at = slice(LANES * c, LANES * c + LANES)
            re, im, bre, bim, are, aim = (
                ref[p, rows, at].astype(jnp.float32) for ref in (own_ref, beside_ref, across_ref) for p in range(2)
            )
            out_ref[0, rows, at] = centre * re - CENTRE[1] * im + (NEAR[0] * bre - NEAR[1] * bim) + FAR * are
            out_ref[1, rows, at] = centre * im + CENTRE[1] * re + (NEAR[0] * bim + NEAR[1] * bre) + FAR * aim


def x_kernel(scalar_ref, mixed_ref, near_ref, fwd_ref, inv_ref, small_ref, rows_ref, out_ref, swept):
    pairs = {}

    def load(g, c):
        at = slice(LANES * c, LANES * c + LANES)
        if g % 2 == 0:
            pairs[c] = near_ref[:, 8 * g : 8 * g + 16, at].astype(jnp.float32)
        rows = slice(8 * g, 8 * g + 8)
        return tuple(mixed_ref[p, rows, at] + pairs[c][p, 8 * (g % 2) : 8 * (g % 2) + 8] for p in range(2))

    def store(g, c, re, im):
        swept[c, 0, 8 * g : 8 * g + 8] = re
        swept[c, 1, 8 * g : 8 * g + 8] = im

    sweep(load, store, scalar_ref[0:1, :], fwd_ref, inv_ref, small_ref, rows_ref, TWIDDLE, 1.0)
    for c in range(COLS):
        tiles = swap_blocks([swept[c, p, 16 * h : 16 * h + 16] for p in range(2) for h in range(2)])
        for q in range(4):
            out_ref[4 * c + q] = tiles[q].astype(jnp.bfloat16)


def y_kernel(scalar_ref, in_ref, fwd_ref, inv_ref, small_ref, rows_ref, out_hbm, field, out_ref, sems):
    for s in range(8):
        flipped = jnp.transpose(in_ref[8 * s : 8 * s + 8].reshape(LANES, LANES)).astype(jnp.float32)
        for p in range(2):
            for x in range(4):
                rows = slice(8 * x, 8 * x + 8)
                low, high = (flipped[64 * p + 32 * h + 8 * x : 64 * p + 32 * h + 8 * x + 8] for h in range(2))
                low, high = exchange(low, high, 64)
                field[p, rows, LANES * (2 * s) : LANES * (2 * s + 1)] = low
                field[p, rows, LANES * (2 * s + 1) : LANES * (2 * s + 2)] = high

    def load(g, c):
        at = slice(LANES * c, LANES * c + LANES)
        return field[0, 8 * g : 8 * g + 8, at], field[1, 8 * g : 8 * g + 8, at]

    def store(g, c, re, im):
        at = slice(LANES * c, LANES * c + LANES)
        out_ref[0, 8 * g : 8 * g + 8, at] = re
        out_ref[1, 8 * g : 8 * g + 8, at] = im

    copies = []

    def send(g):
        rows = slice(8 * g, 8 * g + 8)
        for p in range(2):
            copies.append(pltpu.make_async_copy(out_ref.at[p, rows], out_hbm.at[p, 0, rows], sems.at[g, p]))
            copies[-1].start()

    sweep(load, store, scalar_ref[0:1, :], fwd_ref, inv_ref, small_ref, rows_ref, TWIDDLE_TURNED, -1.0, send)
    for copy in copies:
        copy.wait()


HBM = pl.BlockSpec(memory_space=pltpu.HBM)
VMEM = pl.BlockSpec(memory_space=pltpu.VMEM)
PARAMS = pltpu.CompilerParams(vmem_limit_bytes=48 * 1024 * 1024)


def on_device(wave, potential):
    t = tables()
    f32, bf16 = jnp.float32, jnp.bfloat16
    row_base = lax.axis_index("wa") * ROWS - GRID // 2
    plane = lax.axis_index("gz")
    edge = (plane == 0) | (plane == 7)
    scalars = jnp.stack([row_base.astype(f32) * spacing, jnp.where(edge, CENTRE_EDGE, CENTRE[0])])
    scalars = jnp.broadcast_to(scalars[:, None], (2, LANES))
    own = pl.pallas_call(
        potential_kernel,
        out_shape=jax.ShapeDtypeStruct((2, ROWS, GRID), bf16),
        in_specs=[HBM, HBM],
        out_specs=VMEM,
        scratch_shapes=[
            pltpu.VMEM((2, ROWS, GRID), f32),
            pltpu.VMEM((ROWS, GRID), f32),
            pltpu.SemaphoreType.DMA((4, 2)),
        ],
        compiler_params=PARAMS,
    )(pltpu.with_memory_space_constraint(wave, pltpu.HBM), pltpu.with_memory_space_constraint(potential, pltpu.HBM))
    outward = [(i, i - 1) for i in (2, 4, 6)] + [(i, i + 1) for i in (1, 3, 5)]
    inward = [(i, i + 2) for i in (0, 2, 4)] + [(i, i - 2) for i in (3, 5, 7)]
    beside = lax.ppermute(own, "gz", outward)
    across = lax.ppermute(own, "gz", inward)
    message = pl.pallas_call(
        message_kernel,
        out_shape=jax.ShapeDtypeStruct((2, ROWS, GRID), bf16),
        in_specs=[VMEM, VMEM],
        out_specs=VMEM,
        compiler_params=PARAMS,
    )(own, beside)
    near = lax.ppermute(message, "gz", [(i, i ^ 1) for i in range(8)])
    held = [jnp.asarray(t[name]) for name in ("fwd_x", "inv", "small", "own")]
    mixed = pl.pallas_call(
        mix_kernel,
        out_shape=jax.ShapeDtypeStruct((2, ROWS, GRID), f32),
        in_specs=[VMEM] * 8,
        out_specs=VMEM,
        compiler_params=PARAMS,
    )(scalars, own, beside, across, *held)
    chunks = pl.pallas_call(
        x_kernel,
        out_shape=jax.ShapeDtypeStruct((PARTS_WA, 16, LANES), bf16),
        in_specs=[VMEM] * 7,
        out_specs=VMEM,
        scratch_shapes=[
            pltpu.VMEM((COLS, 2, ROWS, LANES), f32),
        ],
        compiler_params=PARAMS,
    )(scalars, mixed, near, *held)
    chunks = lax.all_to_all(chunks, "wa", 0, 0, tiled=True)
    return pl.pallas_call(
        y_kernel,
        out_shape=jax.ShapeDtypeStruct((2, 1, ROWS, GRID), f32),
        in_specs=[VMEM] * 6,
        out_specs=HBM,
        scratch_shapes=[
            pltpu.VMEM((2, ROWS, GRID), f32),
            pltpu.VMEM((2, ROWS, GRID), f32),
            pltpu.SemaphoreType.DMA((GROUPS, 2)),
        ],
        compiler_params=PARAMS,
    )(scalars, chunks, jnp.asarray(t["fwd_y"]), *held[1:])


def solution(mesh):
    in_specs = (P(None, "gz", "wa", None), P("gz", "wa", None))
    out_specs = P(None, "gz", "wa", None)
    return jax.shard_map(
        on_device, mesh=mesh, in_specs=in_specs, out_specs=out_specs, check_vma=False
    )
```

```python
import math

import jax
import jax.numpy as jnp
import numpy as np
from jax import lax
from jax.experimental import pallas as pl
from jax.experimental.pallas import tpu as pltpu
from jax.sharding import PartitionSpec as P

time_step = 0.001
spacing = 1.0 / 32.0
rotation = 0.9
coupling = 400.0
z_coupling = 0.25

GRID = 2048
LANES = 128
COLS = 16
ROWS = 32
GROUPS = 4
PARTS_WA = 64

NEAR = (2.0 * z_coupling * z_coupling, z_coupling)
FAR = -0.5 * z_coupling * z_coupling
CENTRE = (1.0 - 3.0 * z_coupling * z_coupling, -2.0 * z_coupling)
CENTRE_EDGE = 1.0 - 2.5 * z_coupling * z_coupling


def tables():
    lane = np.arange(LANES)
    turned_lane = 32 * ((lane // 16) % 4) + 16 * (lane // 64) + lane % 16
    scale = 1.0 / math.sqrt(GRID)

    def matrices(order):
        angle = 2.0 * np.pi * ((order[:, None] * lane[None, :]) % LANES) / LANES
        cos, sin = np.cos(angle) * scale, np.sin(angle) * scale
        forward = np.block([[cos, -sin], [sin, cos]])
        return forward

    def split(matrix):
        high = matrix.astype(jnp.bfloat16)
        low = (matrix - high.astype(np.float64)).astype(jnp.bfloat16)
        return np.concatenate([np.asarray(high), np.asarray(low)])

    def twiddle(order):
        angle = 2.0 * np.pi * np.arange(COLS)[:, None] * order[None, :] / GRID
        return np.stack([np.cos(angle), np.sin(angle)]).astype(np.float32)

    angle = 2.0 * np.pi * ((lane[:, None] * lane[None, :]) % LANES) / LANES
    cos, sin = np.cos(angle) * scale, np.sin(angle) * scale
    backward = split(np.block([[cos, sin], [-sin, cos]]))
    mode = np.arange(COLS)[:, None] + COLS * lane[None, :]
    signed = np.where(mode < GRID // 2, mode, mode - GRID).astype(np.float64)
    wavenum = signed * (2.0 * np.pi / (GRID * spacing))
    slope = time_step * rotation * spacing * wavenum
    rows8 = slope[:, None, :] * np.arange(8)[None, :, None]
    own = np.stack([np.cos(rows8), np.sin(rows8)]).astype(np.float32)
    step8 = np.stack([np.cos(8.0 * slope), np.sin(8.0 * slope)]).astype(np.float32)
    return {
        "fwd_x": split(matrices(lane)),
        "fwd_y": split(matrices(turned_lane)),
        "inv": backward,
        "small": np.concatenate([twiddle(lane), twiddle(turned_lane), step8, wavenum[None].astype(np.float32)]),
        "own": own,
    }


TWIDDLE, TWIDDLE_TURNED, STEP8, WAVENUM = 0, 2, 4, 6


SINE = (6.283182621002197, -41.34142303466797, 81.59618377685547, -76.5801010131836, 41.205387115478516, -12.271249771118164)
COSINE = (0.9999992251396179, -19.738983154296875, 64.92872619628906, -85.27239227294922, 58.794029235839844, -21.076766967773438)


def sincos(angle):
    turns = angle * (0.5 / math.pi)
    rest = turns - jnp.floor(turns + 0.5)
    square = rest * rest
    sine, cosine = SINE[-1], COSINE[-1]
    for first, second in zip(SINE[-2::-1], COSINE[-2::-1]):
        sine = sine * square + first
        cosine = cosine * square + second
    return sine * rest, cosine


def dft4(v, sign):
    (ar, ai), (br, bi), (cr, ci), (dr, di) = v
    sr, si, tr, ti = ar + cr, ai + ci, ar - cr, ai - ci
    ur, ui, wr, wi = br + dr, bi + di, br - dr, bi - di
    if sign > 0:
        p, q = (tr + wi, ti - wr), (tr - wi, ti + wr)
    else:
        p, q = (tr - wi, ti + wr), (tr + wi, ti - wr)
    return [(sr + ur, si + ui), p, (sr - ur, si - ui), q]


def turn16(v, power, sign):
    power %= 16
    re, im = v
    if power == 0:
        return v
    c, s = math.cos(2.0 * math.pi * power / 16), -sign * math.sin(2.0 * math.pi * power / 16)
    if power == 4:
        return (im, -re) if sign > 0 else (-im, re)
    if power % 2 == 0:
        h = math.sqrt(0.5)
        return (h * (_pm(re, c) + _pm(im, -s)), h * (_pm(re, s) + _pm(im, c)))
    return (re * c - im * s, re * s + im * c)


def _pm(x, sign):
    return x if sign > 0 else -x


def dft16(v, sign):
    low = [dft4([v[4 * a + b] for a in range(4)], sign) for b in range(4)]
    out = [None] * 16
    for k in range(4):
        high = dft4([turn16(low[b][k], b * k, sign) for b in range(4)], sign)
        for k2 in range(4):
            out[k + 4 * k2] = high[k2]
    return out


def exchange(first, second, width):
    upper = (lax.broadcasted_iota(jnp.int32, first.shape, 1) // width) % 2 == 1
    a = jnp.where(upper, pltpu.roll(second, width, 1), first)
    b = jnp.where(upper, second, pltpu.roll(first, LANES - width, 1))
    return a, b


def swap_blocks(v):
    v0, v2 = exchange(v[0], v[2], 64)
    v1, v3 = exchange(v[1], v[3], 64)
    v0, v1 = exchange(v0, v1, 32)
    v2, v3 = exchange(v2, v3, 32)
    return [v0, v1, v2, v3]


def row_phases(first_row, wavenum, step8, sign):
    angle = time_step * (0.5 * wavenum * wavenum + (sign * rotation * first_row) * wavenum)
    sine, cosine = sincos(angle)
    re, im = cosine, -sine
    sr, si = step8[0], -sign * step8[1]
    out = [(re, im)]
    for _ in range(GROUPS - 1):
        re, im = re * sr - im * si, re * si + im * sr
        out.append((re, im))
    return out


def matrix_stage(re, im, table_ref):
    left = jnp.concatenate(
        [
            jnp.concatenate([jnp.concatenate([group[m] for group in part], axis=0) for part in (re, im)], axis=1)
            for m in range(COLS)
        ],
        axis=0,
    ).astype(jnp.bfloat16)
    left = jnp.concatenate([left, left], axis=1)
    return jnp.dot(left, table_ref[...], preferred_element_type=jnp.float32)


def sweep(load, store, first_row, fwd_ref, inv_ref, small_ref, rows_ref, forward, sign, finish=None):
    phases = row_phases(first_row, small_ref[WAVENUM], small_ref[STEP8 : STEP8 + 2], sign)

    def parts_of(value, m):
        rows = slice(8 * m, 8 * m + 8)
        return value[rows, :LANES], value[rows, LANES:]

    def first(groups):
        re_in, im_in = [], []
        for g in groups:
            out = dft16([load(g, c) for c in range(COLS)], 1)
            for m in range(1, COLS):
                re, im = out[m]
                c, s = small_ref[forward, m : m + 1, :], small_ref[forward + 1, m : m + 1, :]
                out[m] = (re * c + im * s, im * c - re * s)
            re_in.append([v[0] for v in out])
            im_in.append([v[1] for v in out])
        return matrix_stage(re_in, im_in, fwd_ref)

    def second(groups, spectrum):
        re_in, im_in = [[None] * COLS for _ in groups], [[None] * COLS for _ in groups]
        for m in range(COLS):
            own_re, own_im = rows_ref[0, m], -sign * rows_ref[1, m]
            for i, g in enumerate(groups):
                row_re, row_im = phases[g][0][m : m + 1, :], phases[g][1][m : m + 1, :]
                f_re, f_im = own_re * row_re - own_im * row_im, own_re * row_im + own_im * row_re
                re, im = parts_of(spectrum, m)
                re_in[i][m], im_in[i][m] = re * f_re - im * f_im, re * f_im + im * f_re
        return matrix_stage(re_in, im_in, inv_ref)

    def third(groups, turned):
        for i, g in enumerate(groups):
            terms = []
            for m in range(COLS):
                re, im = parts_of(turned, m)
                if m > 0:
                    c, s = small_ref[TWIDDLE, m : m + 1, :], small_ref[TWIDDLE + 1, m : m + 1, :]
                    re, im = re * c - im * s, im * c + re * s
                terms.append((re, im))
            for c, (re, im) in enumerate(dft16(terms, -1)):
                store(g, c, re, im)
            if finish is not None:
                finish(g)

    for g in range(GROUPS):
        groups = (g,)
        third(groups, second(groups, first(groups)))

def potential_kernel(wave_hbm, potential_hbm, out_ref, wave_ref, potential_ref, sems):
    half = GRID // 2
    blocks = [(slice(16 * g, 16 * g + 16), slice(half * h, half * h + half)) for g in range(2) for h in range(2)]
    copies = []
    for b, (rows, at) in enumerate(blocks):
        copies.append([
            pltpu.make_async_copy(wave_hbm.at[:, 0, rows, at], wave_ref.at[:, rows, at], sems.at[b, 0]),
            pltpu.make_async_copy(potential_hbm.at[0, rows, at], potential_ref.at[rows, at], sems.at[b, 1]),
        ])
        for copy in copies[-1]:
            copy.start()
    for (rows, at), waits in zip(blocks, copies):
        for copy in waits:
            copy.wait()
        for first in range(at.start, at.stop, LANES):
            cols = slice(first, first + LANES)
            re, im, pot = wave_ref[0, rows, cols], wave_ref[1, rows, cols], potential_ref[rows, cols]
            sine, cosine = sincos(time_step * (pot + coupling * (re * re + im * im)))
            out_ref[0, rows, cols] = (re * cosine + im * sine).astype(jnp.bfloat16)
            out_ref[1, rows, cols] = (im * cosine - re * sine).astype(jnp.bfloat16)


def message_kernel(own_ref, beside_ref, out_ref):
    re, im = own_ref[0].astype(jnp.float32), own_ref[1].astype(jnp.float32)
    bre, bim = beside_ref[0].astype(jnp.float32), beside_ref[1].astype(jnp.float32)
    out_ref[0] = (NEAR[0] * re - NEAR[1] * im + FAR * bre).astype(jnp.bfloat16)
    out_ref[1] = (NEAR[0] * im + NEAR[1] * re + FAR * bim).astype(jnp.bfloat16)


def mix_kernel(scalar_ref, own_ref, beside_ref, across_ref, *tables_and_out):
    out_ref = tables_and_out[-1]
    centre = scalar_ref[1:2, :]
    for g in range(2):
        rows = slice(16 * g, 16 * g + 16)
        for c in range(COLS):
            at = slice(LANES * c, LANES * c + LANES)
            re, im, bre, bim, are, aim = (
                ref[p, rows, at].astype(jnp.float32) for ref in (own_ref, beside_ref, across_ref) for p in range(2)
            )
            out_ref[0, rows, at] = centre * re - CENTRE[1] * im + (NEAR[0] * bre - NEAR[1] * bim) + FAR * are
            out_ref[1, rows, at] = centre * im + CENTRE[1] * re + (NEAR[0] * bim + NEAR[1] * bre) + FAR * aim


def x_kernel(scalar_ref, mixed_ref, near_ref, fwd_ref, inv_ref, small_ref, rows_ref, out_ref, swept):
    pairs = {}

    def load(g, c):
        at = slice(LANES * c, LANES * c + LANES)
        if g % 2 == 0:
            pairs[c] = near_ref[:, 8 * g : 8 * g + 16, at].astype(jnp.float32)
        rows = slice(8 * g, 8 * g + 8)
        return tuple(mixed_ref[p, rows, at] + pairs[c][p, 8 * (g % 2) : 8 * (g % 2) + 8] for p in range(2))

    def store(g, c, re, im):
        swept[c, 0, 8 * g : 8 * g + 8] = re
        swept[c, 1, 8 * g : 8 * g + 8] = im

    sweep(load, store, scalar_ref[0:1, :], fwd_ref, inv_ref, small_ref, rows_ref, TWIDDLE, 1.0)
    for c in range(COLS):
        tiles = swap_blocks([swept[c, p, 16 * h : 16 * h + 16] for p in range(2) for h in range(2)])
        for q in range(4):
            out_ref[4 * c + q] = tiles[q].astype(jnp.bfloat16)


def y_kernel(scalar_ref, in_ref, fwd_ref, inv_ref, small_ref, rows_ref, out_hbm, field, out_ref, sems):
    for s in range(8):
        flipped = jnp.transpose(in_ref[8 * s : 8 * s + 8].reshape(LANES, LANES)).astype(jnp.float32)
        for p in range(2):
            for x in range(4):
                rows = slice(8 * x, 8 * x + 8)
                low, high = (flipped[64 * p + 32 * h + 8 * x : 64 * p + 32 * h + 8 * x + 8] for h in range(2))
                low, high = exchange(low, high, 64)
                field[p, rows, LANES * (2 * s) : LANES * (2 * s + 1)] = low
                field[p, rows, LANES * (2 * s + 1) : LANES * (2 * s + 2)] = high

    def load(g, c):
        at = slice(LANES * c, LANES * c + LANES)
        return field[0, 8 * g : 8 * g + 8, at], field[1, 8 * g : 8 * g + 8, at]

    def store(g, c, re, im):
        at = slice(LANES * c, LANES * c + LANES)
        out_ref[0, 8 * g : 8 * g + 8, at] = re
        out_ref[1, 8 * g : 8 * g + 8, at] = im

    copies = []

    def send(g):
        rows = slice(8 * g, 8 * g + 8)
        copies.append(pltpu.make_async_copy(out_ref.at[:, rows], out_hbm.at[:, 0, rows], sems.at[g]))
        copies[-1].start()

    sweep(load, store, scalar_ref[0:1, :], fwd_ref, inv_ref, small_ref, rows_ref, TWIDDLE_TURNED, -1.0, send)
    for copy in copies:
        copy.wait()


HBM = pl.BlockSpec(memory_space=pltpu.HBM)
VMEM = pl.BlockSpec(memory_space=pltpu.VMEM)
PARAMS = pltpu.CompilerParams(vmem_limit_bytes=48 * 1024 * 1024)


def on_device(wave, potential):
    t = tables()
    f32, bf16 = jnp.float32, jnp.bfloat16
    row_base = lax.axis_index("wa") * ROWS - GRID // 2
    plane = lax.axis_index("gz")
    edge = (plane == 0) | (plane == 7)
    scalars = jnp.stack([row_base.astype(f32) * spacing, jnp.where(edge, CENTRE_EDGE, CENTRE[0])])
    scalars = jnp.broadcast_to(scalars[:, None], (2, LANES))
    own = pl.pallas_call(
        potential_kernel,
        out_shape=jax.ShapeDtypeStruct((2, ROWS, GRID), bf16),
        in_specs=[HBM, HBM],
        out_specs=VMEM,
        scratch_shapes=[
            pltpu.VMEM((2, ROWS, GRID), f32),
            pltpu.VMEM((ROWS, GRID), f32),
            pltpu.SemaphoreType.DMA((4, 2)),
        ],
        compiler_params=PARAMS,
    )(pltpu.with_memory_space_constraint(wave, pltpu.HBM), pltpu.with_memory_space_constraint(potential, pltpu.HBM))
    outward = [(i, i - 1) for i in (2, 4, 6)] + [(i, i + 1) for i in (1, 3, 5)]
    inward = [(i, i + 2) for i in (0, 2, 4)] + [(i, i - 2) for i in (3, 5, 7)]
    beside = lax.ppermute(own, "gz", outward)
    across = lax.ppermute(own, "gz", inward)
    message = pl.pallas_call(
        message_kernel,
        out_shape=jax.ShapeDtypeStruct((2, ROWS, GRID), bf16),
        in_specs=[VMEM, VMEM],
        out_specs=VMEM,
        compiler_params=PARAMS,
    )(own, beside)
    near = lax.ppermute(message, "gz", [(i, i ^ 1) for i in range(8)])
    held = [jnp.asarray(t[name]) for name in ("fwd_x", "inv", "small", "own")]
    mixed = pl.pallas_call(
        mix_kernel,
        out_shape=jax.ShapeDtypeStruct((2, ROWS, GRID), f32),
        in_specs=[VMEM] * 8,
        out_specs=VMEM,
        compiler_params=PARAMS,
    )(scalars, own, beside, across, *held)
    chunks = pl.pallas_call(
        x_kernel,
        out_shape=jax.ShapeDtypeStruct((PARTS_WA, 16, LANES), bf16),
        in_specs=[VMEM] * 7,
        out_specs=VMEM,
        scratch_shapes=[
            pltpu.VMEM((COLS, 2, ROWS, LANES), f32),
        ],
        compiler_params=PARAMS,
    )(scalars, mixed, near, *held)
    chunks = lax.all_to_all(chunks, "wa", 0, 0, tiled=True)
    return pl.pallas_call(
        y_kernel,
        out_shape=jax.ShapeDtypeStruct((2, 1, ROWS, GRID), f32),
        in_specs=[VMEM] * 6,
        out_specs=HBM,
        scratch_shapes=[
            pltpu.VMEM((2, ROWS, GRID), f32),
            pltpu.VMEM((2, ROWS, GRID), f32),
            pltpu.SemaphoreType.DMA((GROUPS,)),
        ],
        compiler_params=PARAMS,
    )(scalars, chunks, jnp.asarray(t["fwd_y"]), *held[1:])


def solution(mesh):
    in_specs = (P(None, "gz", "wa", None), P("gz", "wa", None))
    out_specs = P(None, "gz", "wa", None)
    return jax.shard_map(
        on_device, mesh=mesh, in_specs=in_specs, out_specs=out_specs, check_vma=False
    )
```

```python
import math

import jax
import jax.numpy as jnp
import numpy as np
from jax import lax
from jax.experimental import pallas as pl
from jax.experimental.pallas import tpu as pltpu
from jax.sharding import PartitionSpec as P

time_step = 0.001
spacing = 1.0 / 32.0
rotation = 0.9
coupling = 400.0
z_coupling = 0.25

GRID = 2048
LANES = 128
COLS = 16
ROWS = 32
GROUPS = 4
PARTS_WA = 64

NEAR = (2.0 * z_coupling * z_coupling, z_coupling)
FAR = -0.5 * z_coupling * z_coupling
CENTRE = (1.0 - 3.0 * z_coupling * z_coupling, -2.0 * z_coupling)
CENTRE_EDGE = 1.0 - 2.5 * z_coupling * z_coupling


def tables():
    lane = np.arange(LANES)
    turned_lane = 32 * ((lane // 16) % 4) + 16 * (lane // 64) + lane % 16
    scale = 1.0 / math.sqrt(GRID)

    def matrices(order):
        angle = 2.0 * np.pi * ((order[:, None] * lane[None, :]) % LANES) / LANES
        cos, sin = np.cos(angle) * scale, np.sin(angle) * scale
        forward = np.block([[cos, -sin], [sin, cos]])
        return forward

    def split(matrix):
        high = matrix.astype(jnp.bfloat16)
        low = (matrix - high.astype(np.float64)).astype(jnp.bfloat16)
        return np.concatenate([np.asarray(high), np.asarray(low)])

    def twiddle(order):
        angle = 2.0 * np.pi * np.arange(COLS)[:, None] * order[None, :] / GRID
        return np.stack([np.cos(angle), np.sin(angle)]).astype(np.float32)

    angle = 2.0 * np.pi * ((lane[:, None] * lane[None, :]) % LANES) / LANES
    cos, sin = np.cos(angle) * scale, np.sin(angle) * scale
    backward = split(np.block([[cos, sin], [-sin, cos]]))
    mode = np.arange(COLS)[:, None] + COLS * lane[None, :]
    signed = np.where(mode < GRID // 2, mode, mode - GRID).astype(np.float64)
    wavenum = signed * (2.0 * np.pi / (GRID * spacing))
    slope = time_step * rotation * spacing * wavenum
    rows8 = slope[:, None, :] * np.arange(8)[None, :, None]
    own = np.stack([np.cos(rows8), np.sin(rows8)]).astype(np.float32)
    step8 = np.stack([np.cos(8.0 * slope), np.sin(8.0 * slope)]).astype(np.float32)
    return {
        "fwd_x": split(matrices(lane)),
        "fwd_y": split(matrices(turned_lane)),
        "inv": backward,
        "small": np.concatenate([twiddle(lane), twiddle(turned_lane), step8, wavenum[None].astype(np.float32)]),
        "own": own,
    }


TWIDDLE, TWIDDLE_TURNED, STEP8, WAVENUM = 0, 2, 4, 6


SINE = (6.283182621002197, -41.34142303466797, 81.59618377685547, -76.5801010131836, 41.205387115478516, -12.271249771118164)
COSINE = (0.9999992251396179, -19.738983154296875, 64.92872619628906, -85.27239227294922, 58.794029235839844, -21.076766967773438)


def sincos(angle):
    turns = angle * (0.5 / math.pi)
    rest = turns - jnp.floor(turns + 0.5)
    square = rest * rest
    sine, cosine = SINE[-1], COSINE[-1]
    for first, second in zip(SINE[-2::-1], COSINE[-2::-1]):
        sine = sine * square + first
        cosine = cosine * square + second
    return sine * rest, cosine


def dft4(v, sign):
    (ar, ai), (br, bi), (cr, ci), (dr, di) = v
    sr, si, tr, ti = ar + cr, ai + ci, ar - cr, ai - ci
    ur, ui, wr, wi = br + dr, bi + di, br - dr, bi - di
    if sign > 0:
        p, q = (tr + wi, ti - wr), (tr - wi, ti + wr)
    else:
        p, q = (tr - wi, ti + wr), (tr + wi, ti - wr)
    return [(sr + ur, si + ui), p, (sr - ur, si - ui), q]


def turn16(v, power, sign):
    power %= 16
    re, im = v
    if power == 0:
        return v
    c, s = math.cos(2.0 * math.pi * power / 16), -sign * math.sin(2.0 * math.pi * power / 16)
    if power == 4:
        return (im, -re) if sign > 0 else (-im, re)
    if power % 2 == 0:
        h = math.sqrt(0.5)
        return (h * (_pm(re, c) + _pm(im, -s)), h * (_pm(re, s) + _pm(im, c)))
    return (re * c - im * s, re * s + im * c)


def _pm(x, sign):
    return x if sign > 0 else -x


def dft16(v, sign):
    low = [dft4([v[4 * a + b] for a in range(4)], sign) for b in range(4)]
    out = [None] * 16
    for k in range(4):
        high = dft4([turn16(low[b][k], b * k, sign) for b in range(4)], sign)
        for k2 in range(4):
            out[k + 4 * k2] = high[k2]
    return out


def exchange(first, second, width):
    upper = (lax.broadcasted_iota(jnp.int32, first.shape, 1) // width) % 2 == 1
    a = jnp.where(upper, pltpu.roll(second, width, 1), first)
    b = jnp.where(upper, second, pltpu.roll(first, LANES - width, 1))
    return a, b


def swap_blocks(v):
    v0, v2 = exchange(v[0], v[2], 64)
    v1, v3 = exchange(v[1], v[3], 64)
    v0, v1 = exchange(v0, v1, 32)
    v2, v3 = exchange(v2, v3, 32)
    return [v0, v1, v2, v3]


def row_phases(first_row, wavenum, step8, sign):
    angle = time_step * (0.5 * wavenum * wavenum + (sign * rotation * first_row) * wavenum)
    sine, cosine = sincos(angle)
    re, im = cosine, -sine
    sr, si = step8[0], -sign * step8[1]
    out = [(re, im)]
    for _ in range(GROUPS - 1):
        re, im = re * sr - im * si, re * si + im * sr
        out.append((re, im))
    return out


def matrix_stage(re, im, table_ref):
    left = jnp.concatenate(
        [
            jnp.concatenate([jnp.concatenate([group[m] for group in part], axis=0) for part in (re, im)], axis=1)
            for m in range(COLS)
        ],
        axis=0,
    ).astype(jnp.bfloat16)
    left = jnp.concatenate([left, left], axis=1)
    return jnp.dot(left, table_ref[...], preferred_element_type=jnp.float32)


def sweep(load, store, first_row, fwd_ref, inv_ref, small_ref, rows_ref, forward, sign, finish=None):
    phases = row_phases(first_row, small_ref[WAVENUM], small_ref[STEP8 : STEP8 + 2], sign)

    def parts_of(value, m):
        rows = slice(8 * m, 8 * m + 8)
        return value[rows, :LANES], value[rows, LANES:]

    def first(groups):
        re_in, im_in = [], []
        for g in groups:
            out = dft16([load(g, c) for c in range(COLS)], 1)
            for m in range(1, COLS):
                re, im = out[m]
                c, s = small_ref[forward, m : m + 1, :], small_ref[forward + 1, m : m + 1, :]
                out[m] = (re * c + im * s, im * c - re * s)
            re_in.append([v[0] for v in out])
            im_in.append([v[1] for v in out])
        return matrix_stage(re_in, im_in, fwd_ref)

    def second(groups, spectrum):
        re_in, im_in = [[None] * COLS for _ in groups], [[None] * COLS for _ in groups]
        for m in range(COLS):
            own_re, own_im = rows_ref[0, m], -sign * rows_ref[1, m]
            for i, g in enumerate(groups):
                row_re, row_im = phases[g][0][m : m + 1, :], phases[g][1][m : m + 1, :]
                f_re, f_im = own_re * row_re - own_im * row_im, own_re * row_im + own_im * row_re
                re, im = parts_of(spectrum, m)
                re_in[i][m], im_in[i][m] = re * f_re - im * f_im, re * f_im + im * f_re
        return matrix_stage(re_in, im_in, inv_ref)

    def third(groups, turned):
        for i, g in enumerate(groups):
            terms = []
            for m in range(COLS):
                re, im = parts_of(turned, m)
                if m > 0:
                    c, s = small_ref[TWIDDLE, m : m + 1, :], small_ref[TWIDDLE + 1, m : m + 1, :]
                    re, im = re * c - im * s, im * c + re * s
                terms.append((re, im))
            for c, (re, im) in enumerate(dft16(terms, -1)):
                store(g, c, re, im)
            if finish is not None:
                finish(g)

    for g in range(GROUPS):
        groups = (g,)
        third(groups, second(groups, first(groups)))

def potential_kernel(wave_hbm, potential_hbm, out_ref, wave_ref, potential_ref, sems):
    half = GRID // 2
    blocks = [(slice(16 * g, 16 * g + 16), slice(half * h, half * h + half)) for g in range(2) for h in range(2)]
    copies = []
    for b, (rows, at) in enumerate(blocks):
        copies.append([
            pltpu.make_async_copy(wave_hbm.at[:, 0, rows, at], wave_ref.at[:, rows, at], sems.at[b, 0]),
            pltpu.make_async_copy(potential_hbm.at[0, rows, at], potential_ref.at[rows, at], sems.at[b, 1]),
        ])
        for copy in copies[-1]:
            copy.start()
    for (rows, at), waits in zip(blocks, copies):
        for copy in waits:
            copy.wait()
        for first in range(at.start, at.stop, LANES):
            cols = slice(first, first + LANES)
            re, im, pot = wave_ref[0, rows, cols], wave_ref[1, rows, cols], potential_ref[rows, cols]
            sine, cosine = sincos(time_step * (pot + coupling * (re * re + im * im)))
            out_ref[0, rows, cols] = (re * cosine + im * sine).astype(jnp.bfloat16)
            out_ref[1, rows, cols] = (im * cosine - re * sine).astype(jnp.bfloat16)


def message_kernel(own_ref, beside_ref, out_ref):
    for g in range(2):
        rows = slice(16 * g, 16 * g + 16)
        for c in range(COLS):
            at = slice(LANES * c, LANES * c + LANES)
            re, im, bre, bim = (ref[p, rows, at].astype(jnp.float32) for ref in (own_ref, beside_ref) for p in range(2))
            out_ref[0, rows, at] = (NEAR[0] * re - NEAR[1] * im + FAR * bre).astype(jnp.bfloat16)
            out_ref[1, rows, at] = (NEAR[0] * im + NEAR[1] * re + FAR * bim).astype(jnp.bfloat16)


def mix_kernel(scalar_ref, own_ref, beside_ref, across_ref, *tables_and_out):
    out_ref = tables_and_out[-1]
    centre = scalar_ref[1:2, :]
    for g in range(2):
        rows = slice(16 * g, 16 * g + 16)
        for c in range(COLS):
            at = slice(LANES * c, LANES * c + LANES)
            re, im, bre, bim, are, aim = (
                ref[p, rows, at].astype(jnp.float32) for ref in (own_ref, beside_ref, across_ref) for p in range(2)
            )
            out_ref[0, rows, at] = centre * re - CENTRE[1] * im + (NEAR[0] * bre - NEAR[1] * bim) + FAR * are
            out_ref[1, rows, at] = centre * im + CENTRE[1] * re + (NEAR[0] * bim + NEAR[1] * bre) + FAR * aim


def x_kernel(scalar_ref, mixed_ref, near_ref, fwd_ref, inv_ref, small_ref, rows_ref, out_ref, swept):
    pairs = {}

    def load(g, c):
        at = slice(LANES * c, LANES * c + LANES)
        if g % 2 == 0:
            pairs[c] = near_ref[:, 8 * g : 8 * g + 16, at].astype(jnp.float32)
        rows = slice(8 * g, 8 * g + 8)
        return tuple(mixed_ref[p, rows, at] + pairs[c][p, 8 * (g % 2) : 8 * (g % 2) + 8] for p in range(2))

    def store(g, c, re, im):
        swept[c, 0, 8 * g : 8 * g + 8] = re
        swept[c, 1, 8 * g : 8 * g + 8] = im

    sweep(load, store, scalar_ref[0:1, :], fwd_ref, inv_ref, small_ref, rows_ref, TWIDDLE, 1.0)
    for c in range(COLS):
        tiles = swap_blocks([swept[c, p, 16 * h : 16 * h + 16] for p in range(2) for h in range(2)])
        for q in range(4):
            out_ref[4 * c + q] = tiles[q].astype(jnp.bfloat16)


def y_kernel(scalar_ref, in_ref, fwd_ref, inv_ref, small_ref, rows_ref, out_hbm, field, out_ref, sems):
    for s in range(8):
        flipped = jnp.transpose(in_ref[8 * s : 8 * s + 8].reshape(LANES, LANES)).astype(jnp.float32)
        for p in range(2):
            for x in range(4):
                rows = slice(8 * x, 8 * x + 8)
                low, high = (flipped[64 * p + 32 * h + 8 * x : 64 * p + 32 * h + 8 * x + 8] for h in range(2))
                low, high = exchange(low, high, 64)
                field[p, rows, LANES * (2 * s) : LANES * (2 * s + 1)] = low
                field[p, rows, LANES * (2 * s + 1) : LANES * (2 * s + 2)] = high

    def load(g, c):
        at = slice(LANES * c, LANES * c + LANES)
        return field[0, 8 * g : 8 * g + 8, at], field[1, 8 * g : 8 * g + 8, at]

    def store(g, c, re, im):
        at = slice(LANES * c, LANES * c + LANES)
        out_ref[0, 8 * g : 8 * g + 8, at] = re
        out_ref[1, 8 * g : 8 * g + 8, at] = im

    copies = []

    def send(g):
        rows = slice(8 * g, 8 * g + 8)
        for p in range(2):
            copies.append(pltpu.make_async_copy(out_ref.at[p, rows], out_hbm.at[p, 0, rows], sems.at[g, p]))
            copies[-1].start()

    sweep(load, store, scalar_ref[0:1, :], fwd_ref, inv_ref, small_ref, rows_ref, TWIDDLE_TURNED, -1.0, send)
    for copy in copies:
        copy.wait()


HBM = pl.BlockSpec(memory_space=pltpu.HBM)
VMEM = pl.BlockSpec(memory_space=pltpu.VMEM)
PARAMS = pltpu.CompilerParams(vmem_limit_bytes=48 * 1024 * 1024)


def on_device(wave, potential):
    t = tables()
    f32, bf16 = jnp.float32, jnp.bfloat16
    row_base = lax.axis_index("wa") * ROWS - GRID // 2
    plane = lax.axis_index("gz")
    edge = (plane == 0) | (plane == 7)
    scalars = jnp.stack([row_base.astype(f32) * spacing, jnp.where(edge, CENTRE_EDGE, CENTRE[0])])
    scalars = jnp.broadcast_to(scalars[:, None], (2, LANES))
    own = pl.pallas_call(
        potential_kernel,
        out_shape=jax.ShapeDtypeStruct((2, ROWS, GRID), bf16),
        in_specs=[HBM, HBM],
        out_specs=VMEM,
        scratch_shapes=[
            pltpu.VMEM((2, ROWS, GRID), f32),
            pltpu.VMEM((ROWS, GRID), f32),
            pltpu.SemaphoreType.DMA((4, 2)),
        ],
        compiler_params=PARAMS,
    )(pltpu.with_memory_space_constraint(wave, pltpu.HBM), pltpu.with_memory_space_constraint(potential, pltpu.HBM))
    outward = [(i, i - 1) for i in (2, 4, 6)] + [(i, i + 1) for i in (1, 3, 5)]
    inward = [(i, i + 2) for i in (0, 2, 4)] + [(i, i - 2) for i in (3, 5, 7)]
    beside = lax.ppermute(own, "gz", outward)
    across = lax.ppermute(own, "gz", inward)
    message = pl.pallas_call(
        message_kernel,
        out_shape=jax.ShapeDtypeStruct((2, ROWS, GRID), bf16),
        in_specs=[VMEM, VMEM],
        out_specs=VMEM,
        compiler_params=PARAMS,
    )(own, beside)
    near = lax.ppermute(message, "gz", [(i, i ^ 1) for i in range(8)])
    held = [jnp.asarray(t[name]) for name in ("fwd_x", "inv", "small", "own")]
    mixed = pl.pallas_call(
        mix_kernel,
        out_shape=jax.ShapeDtypeStruct((2, ROWS, GRID), f32),
        in_specs=[VMEM] * 8,
        out_specs=VMEM,
        compiler_params=PARAMS,
    )(scalars, own, beside, across, *held)
    chunks = pl.pallas_call(
        x_kernel,
        out_shape=jax.ShapeDtypeStruct((PARTS_WA, 16, LANES), bf16),
        in_specs=[VMEM] * 7,
        out_specs=VMEM,
        scratch_shapes=[
            pltpu.VMEM((COLS, 2, ROWS, LANES), f32),
        ],
        compiler_params=PARAMS,
    )(scalars, mixed, near, *held)
    chunks = lax.all_to_all(chunks, "wa", 0, 0, tiled=True)
    return pl.pallas_call(
        y_kernel,
        out_shape=jax.ShapeDtypeStruct((2, 1, ROWS, GRID), f32),
        in_specs=[VMEM] * 6,
        out_specs=HBM,
        scratch_shapes=[
            pltpu.VMEM((2, ROWS, GRID), f32),
            pltpu.VMEM((2, ROWS, GRID), f32),
            pltpu.SemaphoreType.DMA((GROUPS, 2)),
        ],
        compiler_params=PARAMS,
    )(scalars, chunks, jnp.asarray(t["fwd_y"]), *held[1:])


def solution(mesh):
    in_specs = (P(None, "gz", "wa", None), P("gz", "wa", None))
    out_specs = P(None, "gz", "wa", None)
    return jax.shard_map(
        on_device, mesh=mesh, in_specs=in_specs, out_specs=out_specs, check_vma=False
    )
```
